32 devices in a mesh: src: 4 (over y, x), clip: 8 (over z, core).
Axes of the slice: x: 2, y: 2, z: 4, core: 2. Of those that a mesh axis runs over, the one named last changes fastest.
Arguments:
- color_masks: float32 [8, 2, 256, 256], P('clip', None, 'src'), may hold values from -1 to 1
- source_weights: float32 [4], P('src'), may hold values from 0.25 to 4
- pupil_shifts: int32 [4, 2], P('src'), may hold values from 0 to 16
- pupils: float32 [8, 2, 32, 32], replicated, may hold values from -6 to 6
- target_labels: int32 [8, 256, 256], P('clip'), may hold values from 0 to 2, as said below
Outputs:
- mask_grad: float32 [8, 2, 256, 256], P('clip', None, 'src')
- source_grad: float32 [4], P('src')
The draws below stay inside these ranges and needn't reach their ends.
Inputs may be any that keep to these rules, and one draw needn't show every extreme that they name: `target_labels`: 0 marks an uncovered pixel, 1 and 2 the pixels of polygons of the first and of the second color.
All inputs are finite; a program needn't handle non-finite values.
Results may differ from the reference program's by a relative error of at most 0.0003.
Values sent between devices are 32-bit elements; how exact they have to be, the bound alone decides.
A program may use at most 64 MiB of HBM per device.

```python
import math
import jax
import jax.numpy as jnp
from jax import lax

H = 256
K = 48
KP = 32
C = 8
SRC = 4
CLIPS = 8


def draw_target_labels(key, part):
    cover_key, color_key = jax.random.split(key)
    clip_ids = jnp.arange(CLIPS, dtype=jnp.int32)[:, None, None]
    cover_limit = 100 + 900 * clip_ids // max(CLIPS - 1, 1)
    cover_draw = jax.random.randint(cover_key, (CLIPS, H, H), 0, 1000)
    color_ids = jax.random.randint(color_key, (CLIPS, H, H), 1, 3)
    return jnp.where(cover_draw < cover_limit, color_ids, 0).astype(jnp.int32)


def touch_ends(entries, key, smallest, largest):
    longest = entries.shape.index(max(entries.shape))
    spots = []
    for shift in (0, 1):
        where = [jax.random.randint(jax.random.fold_in(key, axis), (), 0, length) for axis, length in enumerate(entries.shape)]
        where[longest] = (where[longest] + shift) % entries.shape[longest]
        spots.append(tuple(where))
    return entries.at[spots[0]].set(smallest).at[spots[1]].set(largest)


def level_of(own_key, dims, cuts, low, largest):
    loudness, own = 1.0, jax.random.fold_in(own_key, 6)
    for position, parts in cuts:
        steps = jnp.exp(jax.random.uniform(jax.random.fold_in(own, position), (parts,), jnp.float32, low / len(cuts), largest / len(cuts)))
        loudness = loudness * jnp.repeat(steps, dims[position] // parts).reshape([-1 if axis == position else 1 for axis in range(len(dims))])
    return loudness


def scatter_about(stream_key, extent, deviation, bound, kind=jnp.bfloat16):
    return jnp.clip(deviation * jax.random.normal(stream_key, extent, jnp.float32), -bound, bound).astype(kind)


def setup_inputs(seed: int = 0) -> dict:
    splits = jax.random.split(jax.random.key(seed), 6)
    color_masks = jnp.clip(jax.random.uniform(splits[0], (CLIPS, 2, H, H), jnp.float32, -1.0, 1.0) * level_of(splits[0], (CLIPS, 2, H, H), ((0, 8), (2, 4)), -0.4, 0.0), -1.0, 1.0)
    source_weights = jnp.clip(jnp.exp(math.log(4.0) - 2.7725887 * jax.random.uniform(splits[1], (SRC,), jnp.float32) ** level_of(splits[1], (SRC,), ((0, 4),), -0.2, 0.2)), 0.25, 4.0)
    pupil_shifts = touch_ends(jax.random.randint(splits[2], (SRC, 2), 0, K - KP + 1), jax.random.fold_in(splits[2], 1), 0, K - KP).astype(jnp.int32)
    pupils = scatter_about(splits[3], (C, 2, KP, KP), 1.0, 6.0, jnp.float32)
    target_labels = draw_target_labels(jax.random.fold_in(splits[5], 71), 0)
    return dict(color_masks=color_masks, source_weights=source_weights, pupil_shifts=pupil_shifts, pupils=pupils, target_labels=target_labels)


steepness = 4.0
threshold = 0.6
loss_weight = 2.0
binarize = 0.25
highest = lax.Precision.HIGHEST

def make_tables(height, band_size, pupil_size):
    pixels = jnp.arange(height, dtype=jnp.int32)
    frequency = jnp.arange(band_size, dtype=jnp.int32) - band_size // 2
    phases = frequency[:, None] * pixels[None, :] % height
    angles = phases.astype(jnp.float32) * (2.0 * math.pi / height)
    scaling = 1.0 / math.sqrt(height * pupil_size)
    forward_cos = jnp.cos(angles) * scaling
    forward_sin = -jnp.sin(angles) * scaling
    pupil_freq = jnp.arange(pupil_size, dtype=jnp.int32) - pupil_size // 2
    back_phases = pixels[:, None] * pupil_freq[None, :] % height
    back_angles = back_phases.astype(jnp.float32) * (2.0 * math.pi / height)
    return (forward_cos, forward_sin, jnp.cos(back_angles), jnp.sin(back_angles))

def matmul(left, right):
    return jnp.dot(left, right, precision=highest, preferred_element_type=jnp.float32)

def contract(form, left, right):
    return jnp.einsum(form, left, right, precision=highest, preferred_element_type=jnp.float32)

def spectrum(field_rows, row_cos, row_sin, col_cos, col_sin):
    cos_part = matmul(field_rows, col_cos.T)
    sin_part = matmul(field_rows, col_sin.T)
    real_part = matmul(row_cos, cos_part) - matmul(row_sin, sin_part)
    imag_part = matmul(row_cos, sin_part) + matmul(row_sin, cos_part)
    return (real_part, imag_part)

def pupil_image(win_real, win_imag, pupils, inverse_cos, inverse_sin):
    pupil_real = pupils[:, 0]
    pupil_imag = pupils[:, 1]
    product_real = pupil_real * win_real[None] - pupil_imag * win_imag[None]
    product_imag = pupil_real * win_imag[None] + pupil_imag * win_real[None]
    half_real = contract('cij,yj->ciy', product_real, inverse_cos) - contract('cij,yj->ciy', product_imag, inverse_sin)
    half_imag = contract('cij,yj->ciy', product_real, inverse_sin) + contract('cij,yj->ciy', product_imag, inverse_cos)
    return (half_real, half_imag)

def field_power(half_real, half_imag, row_cos, row_sin):
    field_real = contract('xi,ciy->cxy', row_cos, half_real) - contract('xi,ciy->cxy', row_sin, half_imag)
    field_imag = contract('xi,ciy->cxy', row_cos, half_imag) + contract('xi,ciy->cxy', row_sin, half_real)
    return lax.optimization_barrier(jnp.sum(field_real * field_real + field_imag * field_imag, axis=0))

def clip_loss(masks_here, source_weights, pupil_shifts, pupils, labels, tables):
    forward_cos, forward_sin, inverse_cos, inverse_sin = tables
    source_count = source_weights.shape[0]
    channels = pupils.shape[0]
    total_loss = jnp.zeros((), jnp.float32)
    for color in range(2):
        spec_real, spec_imag = spectrum(masks_here[color], forward_cos, forward_sin, forward_cos, forward_sin)

        def add_source(summed, inputs):
            weight, shift = inputs
            first = shift[0].astype(jnp.int32)
            second = shift[1].astype(jnp.int32)
            win_real = lax.dynamic_slice(spec_real, (first, second), (KP, KP))
            win_imag = lax.dynamic_slice(spec_imag, (first, second), (KP, KP))
            half_real, half_imag = pupil_image(win_real, win_imag, pupils, inverse_cos, inverse_sin)
            power = field_power(half_real, half_imag, inverse_cos, inverse_sin)
            return (summed + weight * power / (channels * source_count), None)
        intensity, _ = lax.scan(add_source, jnp.zeros((H, H), jnp.float32), (source_weights, pupil_shifts))
        resist = jax.nn.sigmoid(steepness * (intensity - threshold))
        goal = (labels == color + 1).astype(jnp.float32)
        plane = masks_here[color]
        total_loss = total_loss + loss_weight * jnp.sum((resist - goal) ** 2) + binarize * jnp.sum((1.0 - plane * plane) ** 2)
    return total_loss

def reference(color_masks, source_weights, pupil_shifts, pupils, target_labels):
    tables = make_tables(H, K, KP)
    grad_fn = jax.grad(clip_loss, argnums=(0, 1))

    def one_clip(inputs):
        masks_here, labels = inputs
        return grad_fn(masks_here, source_weights, pupil_shifts, pupils, labels, tables)
    mask_grad, weight_grads = lax.map(one_clip, (color_masks, target_labels))
    source_grad = lax.optimization_barrier(jnp.sum(weight_grads, axis=0)) * (SRC / (2.0 * CLIPS * H * H))
    return (mask_grad, source_grad)
```

```python
import functools
import math

import jax
import jax.numpy as jnp
import ml_dtypes
import numpy as np
from jax import lax
from jax.experimental import pallas as pl
from jax.experimental.pallas import tpu as pltpu
from jax.sharding import PartitionSpec as P

K = 48
KP = 32
N = 2 * KP
LANES = 128
HALF = 64

steepness = 4.0
threshold = 0.6
loss_weight = 2.0
binarize = 0.25
f32 = jnp.float32
bf16 = jnp.bfloat16


def halves(table):
    high = table.astype(np.float32).astype(ml_dtypes.bfloat16)
    low = (table - high.astype(np.float64)).astype(np.float32).astype(ml_dtypes.bfloat16)
    return high, low


def beside(table):
    return np.concatenate(halves(table), axis=-1)


def above(table):
    return np.concatenate(halves(table), axis=-2)


def thrice(table):
    high, low = halves(table)
    return np.concatenate([high, low, high], axis=-1)


def spaced(real, imag):
    out = np.zeros((real.shape[0], LANES))
    out[:, : real.shape[1]] = real
    out[:, HALF : HALF + imag.shape[1]] = imag
    return out


def make_tables(height, src_devices):
    rows = height // src_devices
    pixels = np.arange(height)
    angles = 2.0 * np.pi * (((np.arange(K) - K // 2)[:, None] * pixels[None, :]) % height) / height
    scaling = 1.0 / math.sqrt(height * KP)
    fc, fs = np.cos(angles) * scaling, -np.sin(angles) * scaling
    coarse = np.arange(N)
    back = 2.0 * np.pi * ((coarse[:, None] * (np.arange(KP) - KP // 2)[None, :]) % N) / N
    bc, bs = np.cos(back), np.sin(back)
    band = np.arange(1, KP)
    step = height // N
    delta = (pixels[:, None] - step * coarse[None, :]) % height
    up = (1.0 + 2.0 * np.cos(2.0 * np.pi * ((delta[..., None] * band) % height) / height).sum(-1)) / N

    both = np.concatenate([fc, fs], axis=0)
    row_in = np.stack([thrice(both[:, s * rows : (s + 1) * rows]) for s in range(src_devices)])
    col_in = beside(np.concatenate([spaced(fc.T, fs.T), spaced(-fs.T, fc.T)], axis=0))
    half_in = np.zeros((LANES, LANES))
    half_in[:KP] = np.concatenate([bc.T, bs.T], axis=1)
    half_in[HALF : HALF + KP] = np.concatenate([-bs.T, bc.T], axis=1)
    half_in = beside(half_in)
    field_in = thrice(np.concatenate([bc, bs], axis=1))
    up_rows = thrice(up)
    zero = np.zeros_like(up)
    block = np.block([[up, zero], [zero, up]])
    up_cols = beside(block.T)
    down_cols = beside(block)
    down_rows = above(up.T)
    field_back = thrice(np.concatenate([bc.T, bs.T], axis=0))
    half_back = beside(np.concatenate([spaced(bc, -bs), spaced(bs, bc)], axis=0))
    col_back = np.zeros((LANES, 2 * height))
    col_back[:K] = np.concatenate([fc, -fs], axis=1)
    col_back[HALF : HALF + K] = np.concatenate([fs, fc], axis=1)
    col_back = beside(col_back)
    row_back = np.stack([above(both[:, s * rows : (s + 1) * rows].T) for s in range(src_devices)])
    return dict(
        row_in=row_in, col_in=col_in, half_in=half_in, field_in=field_in, up_rows=up_rows, up_cols=up_cols,
        down_cols=down_cols, down_rows=down_rows, field_back=field_back, half_back=half_back,
        col_back=col_back, row_back=row_back,
    )


ORDER = (
    "row_in", "col_in", "half_in", "field_in", "up_rows", "up_cols",
    "down_cols", "down_rows", "field_back", "half_back", "col_back", "row_back",
)
PER_SOURCE = ("row_in", "row_back")


def mm(left, right):
    return jnp.dot(left, right, preferred_element_type=f32)


def split(value):
    high = value.astype(bf16)
    return high, (value - high.astype(f32)).astype(bf16)


def times_table(value, table):
    high, low = split(value)
    width = table.shape[1] // 2
    first = mm(high, table[:, :width]) + mm(high, table[:, width:])
    return first + mm(low, table[:, :width])


def table_times(table, value):
    high, low = split(value)
    height = table.shape[0] // 2
    first = mm(table, high)
    return first[:height] + first[height:] + mm(table[:height], low)


def table_thrice(table, value):
    high, low = split(value)
    return mm(table, jnp.concatenate([high, high, low], axis=0))


def kernel(
    src_devices, clip_devices, scale,
    shifts, weights, masks_hbm, pupils_hbm, labels_hbm, *rest,
):
    count = len(ORDER)
    table_hbm = dict(zip(ORDER, rest[:count]))
    mask_out, term_out = rest[count : count + 2]
    tables = dict(zip(ORDER, rest[count + 2 : 2 * count + 2]))
    (
        masks, pupils, labels, pupil_real, pupil_imag, fields, padded, total,
        spec_slots, power_slots, grad_slots, term_slots,
        local_sems, spec_send, spec_recv, power_send, power_recv,
        grad_send, grad_recv, term_send, term_recv,
    ) = rest[2 * count + 2 :]
    me = lax.axis_index("src")
    my_clip = lax.axis_index("clip")

    def bring(name):
        source = table_hbm[name]
        if name in PER_SOURCE:
            source = source.at[me]
        return pltpu.make_async_copy(source, tables[name], local_sems.at[ORDER.index(name)])

    copy_masks = pltpu.make_async_copy(masks_hbm, masks, local_sems.at[count])
    copy_pupils = pltpu.make_async_copy(pupils_hbm, pupils, local_sems.at[count + 1])
    copy_labels = pltpu.make_async_copy(labels_hbm, labels, local_sems.at[count + 2])
    copies = {name: bring(name) for name in ORDER}
    copy_masks.start()
    copies["row_in"].start()
    copies["col_in"].start()
    copy_pupils.start()
    for name in ORDER[2:6]:
        copies[name].start()
    copy_labels.start()
    for name in ORDER[6:]:
        copies[name].start()

    barrier = pltpu.get_barrier_semaphore()
    for d in range(1, src_devices):
        pl.semaphore_signal(
            barrier, inc=1, device_id={"src": lax.rem(me + d, src_devices)}, device_id_type=pl.DeviceIdType.MESH
        )
    for d in range(1, clip_devices):
        pl.semaphore_signal(
            barrier, inc=1, device_id={"clip": lax.rem(my_clip + d, clip_devices)},
            device_id_type=pl.DeviceIdType.MESH,
        )

    def exchange(axis, devices, mine, slots, send, recv):
        sent = []
        for d in range(1, devices):
            copy = pltpu.make_async_remote_copy(
                src_ref=slots.at[mine], dst_ref=slots.at[mine],
                send_sem=send.at[d - 1], recv_sem=recv.at[d - 1],
                device_id={axis: lax.rem(mine + d, devices)}, device_id_type=pl.DeviceIdType.MESH,
            )
            copy.start()
            sent.append(copy)
        return sent

    def arrive(sent):
        for copy in sent:
            copy.wait_recv()

    def add_slots(slots, devices):
        value = slots[0]
        for d in range(1, devices):
            value = value + slots[d]
        return value

    lane = lax.broadcasted_iota(jnp.int32, (1, LANES), 1)
    low_half = lane < HALF
    sign = jnp.where(low_half, -1.0, 1.0).astype(f32)

    def rotate(value):
        return pltpu.roll(value, HALF, 1) * sign

    copy_masks.wait()
    copies["row_in"].wait()
    copies["col_in"].wait()
    height = masks.shape[2]
    both_masks = jnp.concatenate([masks[0], masks[1]], axis=1)
    rows_done = table_thrice(tables["row_in"][...], both_masks)
    stacked = jnp.concatenate(
        [
            jnp.concatenate([rows_done[:K, c * height : (c + 1) * height], rows_done[K:, c * height : (c + 1) * height]], axis=1)
            for c in range(2)
        ],
        axis=0,
    )
    spec_slots[me] = times_table(stacked, tables["col_in"][...])
    pl.semaphore_wait(barrier, src_devices + clip_devices - 2)
    spec_sent = exchange("src", src_devices, me, spec_slots, spec_send, spec_recv)

    copy_pupils.wait()
    channels = pupils.shape[0]
    blank = jnp.zeros((KP, HALF - KP), f32)
    for c in range(channels):
        pr, pi = pupils[c, 0], pupils[c, 1]
        pupil_real[c] = jnp.concatenate([pr, blank, pr, blank], axis=1)
        pupil_imag[c] = jnp.concatenate([pi, blank, pi, blank], axis=1)
    padded[...] = jnp.zeros_like(padded)
    first = shifts[0, 0]
    second = shifts[0, 1]
    weight = weights[0]
    copies["half_in"].wait()
    copies["field_in"].wait()

    arrive(spec_sent)
    total[...] = add_slots(spec_slots, src_devices)
    products = []
    for k in range(2):
        window = pltpu.roll(total[pl.ds(first + k * K, KP), :], lax.rem(LANES - second, LANES), 1)
        turned = rotate(window)
        for c in range(channels):
            products.append(pupil_real[c] * window + pupil_imag[c] * turned)
    half = times_table(jnp.concatenate(products, axis=0), tables["half_in"][...])
    half_high, half_low = split(half)
    turn_high, turn_low = split(rotate(half))
    columns = []
    for b in range(2 * channels):
        rows = slice(b * KP, (b + 1) * KP)
        columns.append(
            jnp.concatenate(
                [half_high[rows], turn_high[rows], half_high[rows], turn_high[rows], half_low[rows], turn_low[rows]],
                axis=0,
            )
        )
    power = []
    for k in range(2):
        wide = mm(tables["field_in"][...], jnp.concatenate(columns[k * channels : (k + 1) * channels], axis=1))
        fields[k] = wide
        squares = wide * wide
        summed = squares[:, :LANES]
        for c in range(1, channels):
            summed = summed + squares[:, c * LANES : (c + 1) * LANES]
        power.append(summed + pltpu.roll(summed, HALF, 1))
    raw = jnp.where(low_half, power[0], power[1]) * (1.0 / (channels * src_devices))
    power_slots[me] = raw * weight
    power_sent = exchange("src", src_devices, me, power_slots, power_send, power_recv)
    copies["up_rows"].wait()
    copies["up_cols"].wait()
    copy_labels.wait()
    for name in ORDER[6:]:
        copies[name].wait()
    arrive(power_sent)

    coarse = add_slots(power_slots, src_devices)
    tall = table_thrice(tables["up_rows"][...], coarse)
    chunk = HALF
    thin = []
    for r in range(0, height, chunk):
        intensity = times_table(tall[r : r + chunk], tables["up_cols"][...])
        resist = 1.0 / (1.0 + jnp.exp(-steepness * (intensity - threshold)))
        codes = labels[r : r + chunk, :]
        goal = jnp.concatenate([jnp.where(codes == 1, 1.0, 0.0), jnp.where(codes == 2, 1.0, 0.0)], axis=1).astype(f32)
        slope = (2.0 * loss_weight * steepness) * (resist - goal) * resist * (1.0 - resist)
        thin.append(times_table(slope, tables["down_cols"][...]))
    slope = table_times(tables["down_rows"][...], jnp.concatenate(thin, axis=0))

    term = jnp.sum(slope * raw, axis=0, keepdims=True)
    term_slots[my_clip] = jnp.broadcast_to(jnp.sum(term, axis=1, keepdims=True), (8, LANES))
    term_sent = exchange("clip", clip_devices, my_clip, term_slots, term_send, term_recv)

    slope = slope * (weight * (2.0 / (channels * src_devices)))
    swapped = pltpu.roll(slope, HALF, 1)
    doubled = [jnp.where(low_half, slope, swapped), jnp.where(low_half, swapped, slope)]
    pieces = []
    for k in range(2):
        field_grad = fields[k] * jnp.concatenate([doubled[k]] * channels, axis=1)
        back = table_thrice(tables["field_back"][...], field_grad)
        for c in range(channels):
            block = back[:, c * LANES : (c + 1) * LANES]
            pieces.append(block[:KP] - rotate(block[KP:]))
    product_grad = times_table(jnp.concatenate(pieces, axis=0), tables["half_back"][...])
    for k in range(2):
        along = jnp.zeros((KP, LANES), f32)
        across = jnp.zeros((KP, LANES), f32)
        for c in range(channels):
            b = k * channels + c
            block = product_grad[b * KP : (b + 1) * KP]
            along = along + pupil_real[c] * block
            across = across + pupil_imag[c] * block
        window_grad = along - rotate(across)
        padded[k, K - KP : K, :] = pltpu.roll(window_grad, second, 1)
    grad_slots[me] = jnp.concatenate([padded[k, pl.ds(K - KP - first, K), :] for k in range(2)], axis=0)
    grad_sent = exchange("src", src_devices, me, grad_slots, grad_send, grad_recv)

    arrive(term_sent)
    term_out[...] = add_slots(term_slots, clip_devices) * scale
    arrive(grad_sent)
    spread = times_table(add_slots(grad_slots, src_devices), tables["col_back"][...])
    width = 2 * height
    folded = jnp.concatenate(
        [
            jnp.concatenate([spread[:K, :height], spread[K:, :height]], axis=1),
            jnp.concatenate([spread[:K, height:width], spread[K:, height:width]], axis=1),
        ],
        axis=0,
    )
    grad = table_times(tables["row_back"][...], folded)
    mask_out[0] = grad[:, :height]
    mask_out[1] = grad[:, height:]
    for copy in spec_sent + power_sent + term_sent + grad_sent:
        copy.wait_send()


def per_device(color_masks, source_weights, pupil_shifts, pupils, target_labels):
    src_devices = lax.axis_size("src")
    clip_devices = lax.axis_size("clip")
    rows, height = color_masks.shape[2], color_masks.shape[3]
    channels = pupils.shape[0]
    tables = make_tables(height, src_devices)
    masks_here = color_masks[0]
    scale = src_devices / (2.0 * clip_devices * height * height)
    operands = [jnp.asarray(tables[name]) for name in ORDER]
    table_scratch = []
    for name in ORDER:
        shape = tables[name].shape[1:] if name in PER_SOURCE else tables[name].shape
        table_scratch.append(pltpu.VMEM(shape, bf16))
    smem = pl.BlockSpec(memory_space=pltpu.SMEM)
    far = pl.BlockSpec(memory_space=pl.ANY)
    near = pl.BlockSpec(memory_space=pltpu.VMEM)
    dma = pltpu.SemaphoreType.DMA
    mask_grad, terms = pl.pallas_call(
        functools.partial(kernel, src_devices, clip_devices, scale),
        out_shape=(
            jax.ShapeDtypeStruct((2, rows, height), f32),
            jax.ShapeDtypeStruct((8, LANES), f32),
        ),
        in_specs=[smem, smem] + [far] * (3 + len(ORDER)),
        out_specs=(near, near),
        scratch_shapes=table_scratch
        + [
            pltpu.VMEM((2, rows, height), f32),
            pltpu.VMEM(pupils.shape, f32),
            pltpu.VMEM((height, height), jnp.int32),
            pltpu.VMEM((channels, KP, LANES), f32),
            pltpu.VMEM((channels, KP, LANES), f32),
            pltpu.VMEM((2, N, channels * LANES), f32),
            pltpu.VMEM((2, 2 * K - KP, LANES), f32),
            pltpu.VMEM((2 * K, LANES), f32),
            pltpu.VMEM((src_devices, 2 * K, LANES), f32),
            pltpu.VMEM((src_devices, N, LANES), f32),
            pltpu.VMEM((src_devices, 2 * K, LANES), f32),
            pltpu.VMEM((clip_devices, 8, LANES), f32),
            dma((len(ORDER) + 3,)),
        ]
        + [dma((src_devices - 1,))] * 6
        + [dma((clip_devices - 1,))] * 2,
        compiler_params=pltpu.CompilerParams(
            collective_id=0, has_side_effects=True, vmem_limit_bytes=32 * 1024 * 1024
        ),
        name="abbe_gradient",
    )(pupil_shifts, source_weights, masks_here, pupils, target_labels[0], *operands)
    mask_grad = mask_grad - (4.0 * binarize) * (1.0 - masks_here * masks_here) * masks_here
    return mask_grad[None], terms[0, :1]


def solution(mesh):
    in_specs = (P("clip", None, "src", None), P("src"), P("src", None), P(), P("clip", None, None))
    out_specs = (P("clip", None, "src", None), P("src"))
    return jax.shard_map(
        per_device, mesh=mesh, in_specs=in_specs, out_specs=out_specs, check_vma=False
    )
```

```python
import functools
import math

import jax
import jax.numpy as jnp
import ml_dtypes
import numpy as np
from jax import lax
from jax.experimental import pallas as pl
from jax.experimental.pallas import tpu as pltpu
from jax.sharding import PartitionSpec as P

K = 48
KP = 32
N = 2 * KP
LANES = 128
HALF = 64
CHUNK = 64

steepness = 4.0
threshold = 0.6
loss_weight = 2.0
binarize = 0.25
f32 = jnp.float32
bf16 = jnp.bfloat16


def halves(table):
    high = table.astype(np.float32).astype(ml_dtypes.bfloat16)
    low = (table - high.astype(np.float64)).astype(np.float32).astype(ml_dtypes.bfloat16)
    return high, low


def beside(table):
    return np.concatenate(halves(table), axis=-1)


def above(table):
    return np.concatenate(halves(table), axis=-2)


def thrice(table):
    high, low = halves(table)
    return np.concatenate([high, low, high], axis=-1)


def spaced(real, imag):
    out = np.zeros((real.shape[0], LANES))
    out[:, : real.shape[1]] = real
    out[:, HALF : HALF + imag.shape[1]] = imag
    return out


def make_tables(height, src_devices):
    rows = height // src_devices
    pixels = np.arange(height)
    angles = 2.0 * np.pi * (((np.arange(K) - K // 2)[:, None] * pixels[None, :]) % height) / height
    scaling = 1.0 / math.sqrt(height * KP)
    fc, fs = np.cos(angles) * scaling, -np.sin(angles) * scaling
    coarse = np.arange(N)
    back = 2.0 * np.pi * ((coarse[:, None] * (np.arange(KP) - KP // 2)[None, :]) % N) / N
    bc, bs = np.cos(back), np.sin(back)
    band = np.arange(1, KP)
    step = height // N
    delta = (pixels[:, None] - step * coarse[None, :]) % height
    up = (1.0 + 2.0 * np.cos(2.0 * np.pi * ((delta[..., None] * band) % height) / height).sum(-1)) / N

    both = np.concatenate([fc, fs], axis=0)
    row_in = np.stack([thrice(both[:, s * rows : (s + 1) * rows]) for s in range(src_devices)])
    col_in = beside(np.concatenate([spaced(fc.T, fs.T), spaced(-fs.T, fc.T)], axis=0))
    half_in = np.zeros((LANES, LANES))
    half_in[:KP] = np.concatenate([bc.T, bs.T], axis=1)
    half_in[HALF : HALF + KP] = np.concatenate([-bs.T, bc.T], axis=1)
    half_in = beside(half_in)
    field_in = thrice(np.concatenate([bc, bs], axis=1))
    up_rows = thrice(up)
    up_cols = beside(np.concatenate([up.T, np.zeros_like(up.T)], axis=0))
    down_cols = beside(np.concatenate([up, up], axis=1))
    down_rows = above(up.T)
    field_back = thrice(np.concatenate([bc.T, bs.T], axis=0))
    half_back = beside(np.concatenate([spaced(bc, -bs), spaced(bs, bc)], axis=0))
    col_back = np.zeros((LANES, 2 * height))
    col_back[:K] = np.concatenate([fc, -fs], axis=1)
    col_back[HALF : HALF + K] = np.concatenate([fs, fc], axis=1)
    col_back = beside(col_back)
    row_back = np.stack([above(both[:, s * rows : (s + 1) * rows].T) for s in range(src_devices)])
    return dict(
        row_in=row_in, col_in=col_in, half_in=half_in, field_in=field_in, up_rows=up_rows, up_cols=up_cols,
        down_cols=down_cols, down_rows=down_rows, field_back=field_back, half_back=half_back,
        col_back=col_back, row_back=row_back,
    )


ORDER = (
    "row_in", "col_in", "half_in", "field_in", "up_rows", "up_cols",
    "down_cols", "down_rows", "field_back", "half_back", "col_back", "row_back",
)
PER_SOURCE = ("row_in", "row_back")


def mm(left, right):
    return jnp.dot(left, right, preferred_element_type=f32)


def split(value):
    high = value.astype(bf16)
    return high, (value - high.astype(f32)).astype(bf16)


def times_table(value, table):
    high, low = split(value)
    width = table.shape[1] // 2
    first = mm(high, table[:, :width]) + mm(high, table[:, width:])
    return first + mm(low, table[:, :width])


def table_times(table, value):
    high, low = split(value)
    height = table.shape[0] // 2
    first = mm(table, high)
    return first[:height] + first[height:] + mm(table[:height], low)


def table_thrice(table, value):
    high, low = split(value)
    return mm(table, jnp.concatenate([high, high, low], axis=0))


def kernel(
    src_devices, clip_devices, scale,
    shifts_hbm, weights_hbm, masks_hbm, pupils_hbm, labels_hbm, *rest,
):
    count = len(ORDER)
    table_hbm = dict(zip(ORDER, rest[:count]))
    mask_out, term_out = rest[count : count + 2]
    tables = dict(zip(ORDER, rest[count + 2 : 2 * count + 2]))
    (
        shifts, weights, masks, pupils, labels, pupil_real, pupil_imag, fields, padded, total,
        spec_slots, power_slots, grad_slots, term_slots,
        local_sems, spec_send, spec_recv, power_send, power_recv,
        grad_send, grad_recv, term_send, term_recv,
    ) = rest[2 * count + 2 :]
    me = lax.axis_index("src")
    my_clip = lax.axis_index("clip")

    def bring(name):
        source = table_hbm[name]
        if name in PER_SOURCE:
            source = source.at[me]
        return pltpu.make_async_copy(source, tables[name], local_sems.at[ORDER.index(name)])

    copy_masks = pltpu.make_async_copy(masks_hbm, masks, local_sems.at[count])
    copy_pupils = pltpu.make_async_copy(pupils_hbm, pupils, local_sems.at[count + 1])
    copy_labels = pltpu.make_async_copy(labels_hbm, labels, local_sems.at[count + 2])
    copy_shifts = pltpu.make_async_copy(shifts_hbm, shifts, local_sems.at[count + 3])
    copy_weights = pltpu.make_async_copy(weights_hbm, weights, local_sems.at[count + 4])
    copies = {name: bring(name) for name in ORDER}
    copy_masks.start()
    copies["row_in"].start()
    copies["col_in"].start()
    copy_pupils.start()
    copy_shifts.start()
    copy_weights.start()
    for name in ORDER[2:6]:
        copies[name].start()
    copy_labels.start()
    for name in ORDER[6:]:
        copies[name].start()

    barrier = pltpu.get_barrier_semaphore()
    for d in range(1, src_devices):
        pl.semaphore_signal(
            barrier, inc=1, device_id={"src": lax.rem(me + d, src_devices)}, device_id_type=pl.DeviceIdType.MESH
        )
    for d in range(1, clip_devices):
        pl.semaphore_signal(
            barrier, inc=1, device_id={"clip": lax.rem(my_clip + d, clip_devices)},
            device_id_type=pl.DeviceIdType.MESH,
        )

    def exchange(axis, devices, mine, slots, send, recv):
        sent = []
        for d in range(1, devices):
            copy = pltpu.make_async_remote_copy(
                src_ref=slots.at[mine], dst_ref=slots.at[mine],
                send_sem=send.at[d - 1], recv_sem=recv.at[d - 1],
                device_id={axis: lax.rem(mine + d, devices)}, device_id_type=pl.DeviceIdType.MESH,
            )
            copy.start()
            sent.append(copy)
        return sent

    def arrive(sent):
        for copy in sent:
            copy.wait_recv()

    def add_slots(slots, devices):
        value = slots[0]
        for d in range(1, devices):
            value = value + slots[d]
        return value

    lane = lax.broadcasted_iota(jnp.int32, (1, LANES), 1)
    low_half = lane < HALF
    sign = jnp.where(low_half, -1.0, 1.0).astype(f32)

    def rotate(value):
        return pltpu.roll(value, HALF, 1) * sign

    copy_masks.wait()
    copies["row_in"].wait()
    copies["col_in"].wait()
    height = masks.shape[2]
    colors = range(2)
    spec_sent, power_sent, grad_sent = [], [], []
    for k in colors:
        rows_done = table_thrice(tables["row_in"][...], masks[k])
        stacked = jnp.concatenate([rows_done[:K], rows_done[K:]], axis=1)
        spec_slots[k, me] = times_table(stacked, tables["col_in"][...])
        if k == 0:
            pl.semaphore_wait(barrier, src_devices + clip_devices - 2)
        spec_sent.append(
            exchange("src", src_devices, me, spec_slots.at[k], spec_send.at[k], spec_recv.at[k])
        )

    copy_pupils.wait()
    channels = pupils.shape[0]
    blank = jnp.zeros((KP, HALF - KP), f32)
    for c in range(channels):
        pr, pi = pupils[c, 0], pupils[c, 1]
        pupil_real[c] = jnp.concatenate([pr, blank, pr, blank], axis=1)
        pupil_imag[c] = jnp.concatenate([pi, blank, pi, blank], axis=1)
    padded[...] = jnp.zeros_like(padded)
    copy_shifts.wait()
    copy_weights.wait()
    first = shifts[0, 0]
    second = shifts[0, 1]
    weight = weights[0, 0]
    copies["half_in"].wait()
    copies["field_in"].wait()

    raw = []
    for k in colors:
        arrive(spec_sent[k])
        total[k] = add_slots(spec_slots.at[k], src_devices)
        window = pltpu.roll(total[k, pl.ds(first, KP), :], lax.rem(LANES - second, LANES), 1)
        turned = rotate(window)
        products = [pupil_real[c] * window + pupil_imag[c] * turned for c in range(channels)]
        half = times_table(jnp.concatenate(products, axis=0), tables["half_in"][...])
        half_high, half_low = split(half)
        turn_high, turn_low = split(rotate(half))
        columns = []
        for c in range(channels):
            rows = slice(c * KP, (c + 1) * KP)
            columns.append(
                jnp.concatenate(
                    [half_high[rows], turn_high[rows], half_high[rows], turn_high[rows], half_low[rows], turn_low[rows]],
                    axis=0,
                )
            )
        wide = mm(tables["field_in"][...], jnp.concatenate(columns, axis=1))
        fields[k] = wide
        squares = wide * wide
        summed = squares[:, :LANES]
        for c in range(1, channels):
            summed = summed + squares[:, c * LANES : (c + 1) * LANES]
        power = (summed + pltpu.roll(summed, HALF, 1)) * (1.0 / (channels * src_devices))
        raw.append(power)
        power_slots[k, me] = jnp.where(low_half, power[: N // 2], power[N // 2 :]) * weight
        power_sent.append(
            exchange("src", src_devices, me, power_slots.at[k], power_send.at[k], power_recv.at[k])
        )
    copies["up_rows"].wait()
    copies["up_cols"].wait()
    copy_labels.wait()
    for name in ORDER[6:]:
        copies[name].wait()

    term = jnp.zeros((1, LANES), f32)
    for k in colors:
        arrive(power_sent[k])
        packed = add_slots(power_slots.at[k], src_devices)
        coarse = jnp.concatenate([packed, pltpu.roll(packed, HALF, 1)], axis=0)
        tall = table_thrice(tables["up_rows"][...], coarse)
        thin = []
        for r in range(0, height, CHUNK):
            intensity = times_table(tall[r : r + CHUNK], tables["up_cols"][...])
            level = jnp.tanh((0.5 * steepness) * (intensity - threshold))
            shifted = level + jnp.where(labels[r : r + CHUNK, :] == k + 1, -1.0, 1.0)
            slope = (0.25 * loss_weight * steepness) * shifted * (1.0 - level * level)
            thin.append(times_table(slope, tables["down_cols"][...]))
        slope = table_times(tables["down_rows"][...], jnp.concatenate(thin, axis=0))
        term = term + jnp.sum(slope * raw[k], axis=0, keepdims=True)
        if k == 1:
            term_slots[my_clip] = jnp.broadcast_to(0.5 * jnp.sum(term, axis=1, keepdims=True), (8, LANES))
            term_sent = exchange("clip", clip_devices, my_clip, term_slots, term_send, term_recv)

        slope = slope * (weight * (2.0 / (channels * src_devices)))
        field_grad = fields[k] * jnp.concatenate([slope] * channels, axis=1)
        back = table_thrice(tables["field_back"][...], field_grad)
        pieces = []
        for c in range(channels):
            block = back[:, c * LANES : (c + 1) * LANES]
            pieces.append(block[:KP] - rotate(block[KP:]))
        product_grad = times_table(jnp.concatenate(pieces, axis=0), tables["half_back"][...])
        along = jnp.zeros((KP, LANES), f32)
        across = jnp.zeros((KP, LANES), f32)
        for c in range(channels):
            block = product_grad[c * KP : (c + 1) * KP]
            along = along + pupil_real[c] * block
            across = across + pupil_imag[c] * block
        window_grad = along - rotate(across)
        padded[k, K - KP : K, :] = pltpu.roll(window_grad, second, 1)
        grad_slots[k, me] = padded[k, pl.ds(K - KP - first, K), :]
        grad_sent.append(
            exchange("src", src_devices, me, grad_slots.at[k], grad_send.at[k], grad_recv.at[k])
        )

    for k in colors:
        arrive(grad_sent[k])
        spread = times_table(add_slots(grad_slots.at[k], src_devices), tables["col_back"][...])
        folded = jnp.concatenate([spread[:, :height], spread[:, height:]], axis=0)
        mask_out[k] = table_times(tables["row_back"][...], folded)
    arrive(term_sent)
    term_out[...] = add_slots(term_slots, clip_devices) * scale
    for sent in spec_sent + power_sent + [term_sent] + grad_sent:
        for copy in sent:
            copy.wait_send()


def per_device(color_masks, source_weights, pupil_shifts, pupils, target_labels):
    src_devices = lax.axis_size("src")
    clip_devices = lax.axis_size("clip")
    rows, height = color_masks.shape[2], color_masks.shape[3]
    channels = pupils.shape[0]
    tables = make_tables(height, src_devices)
    masks_here = color_masks[0]
    scale = src_devices / (2.0 * clip_devices * height * height)
    operands = [jnp.asarray(tables[name]) for name in ORDER]
    table_scratch = []
    for name in ORDER:
        shape = tables[name].shape[1:] if name in PER_SOURCE else tables[name].shape
        table_scratch.append(pltpu.VMEM(shape, bf16))
    far = pl.BlockSpec(memory_space=pltpu.HBM)
    near = pl.BlockSpec(memory_space=pltpu.VMEM)
    dma = pltpu.SemaphoreType.DMA
    mask_grad, terms = pl.pallas_call(
        functools.partial(kernel, src_devices, clip_devices, scale),
        out_shape=(
            jax.ShapeDtypeStruct((2, rows, height), f32),
            jax.ShapeDtypeStruct((8, LANES), f32),
        ),
        in_specs=[far] * (5 + len(ORDER)),
        out_specs=(near, near),
        scratch_shapes=table_scratch
        + [
            pltpu.SMEM((1, 2), jnp.int32),
            pltpu.SMEM((1, 1), f32),
            pltpu.VMEM((2, rows, height), f32),
            pltpu.VMEM(pupils.shape, f32),
            pltpu.VMEM((height, height), jnp.int32),
            pltpu.VMEM((channels, KP, LANES), f32),
            pltpu.VMEM((channels, KP, LANES), f32),
            pltpu.VMEM((2, N, channels * LANES), f32),
            pltpu.VMEM((2, 2 * K - KP, LANES), f32),
            pltpu.VMEM((2, K, LANES), f32),
            pltpu.VMEM((2, src_devices, K, LANES), f32),
            pltpu.VMEM((2, src_devices, N // 2, LANES), f32),
            pltpu.VMEM((2, src_devices, K, LANES), f32),
            pltpu.VMEM((clip_devices, 8, LANES), f32),
            dma((len(ORDER) + 5,)),
        ]
        + [dma((2, src_devices - 1))] * 6
        + [dma((clip_devices - 1,))] * 2,
        compiler_params=pltpu.CompilerParams(
            collective_id=0, has_side_effects=True, vmem_limit_bytes=60 * 1024 * 1024
        ),
        name="abbe_gradient",
    )(pupil_shifts, source_weights[None], masks_here, pupils, target_labels[0], *operands)
    mask_grad = mask_grad - (4.0 * binarize) * (1.0 - masks_here * masks_here) * masks_here
    return mask_grad[None], terms[0, :1]


def solution(mesh):
    in_specs = (P("clip", None, "src", None), P("src"), P("src", None), P(), P("clip", None, None))
    out_specs = (P("clip", None, "src", None), P("src"))
    return jax.shard_map(
        per_device, mesh=mesh, in_specs=in_specs, out_specs=out_specs, check_vma=False
    )
```

```python
import functools
import math

import jax
import jax.numpy as jnp
import ml_dtypes
import numpy as np
from jax import lax
from jax.experimental import pallas as pl
from jax.experimental.pallas import tpu as pltpu
from jax.sharding import PartitionSpec as P

K = 48
KP = 32
N = 2 * KP
LANES = 128
HALF = 64
CHUNK = 64

steepness = 4.0
threshold = 0.6
loss_weight = 2.0
binarize = 0.25
f32 = jnp.float32
bf16 = jnp.bfloat16


def halves(table):
    high = table.astype(np.float32).astype(ml_dtypes.bfloat16)
    low = (table - high.astype(np.float64)).astype(np.float32).astype(ml_dtypes.bfloat16)
    return high, low


def beside(table):
    return np.concatenate(halves(table), axis=-1)


def above(table):
    return np.concatenate(halves(table), axis=-2)


def thrice(table):
    high, low = halves(table)
    return np.concatenate([high, low, high], axis=-1)


def spaced(real, imag):
    out = np.zeros((real.shape[0], LANES))
    out[:, : real.shape[1]] = real
    out[:, HALF : HALF + imag.shape[1]] = imag
    return out


def make_tables(height, src_devices):
    rows = height // src_devices
    pixels = np.arange(height)
    angles = 2.0 * np.pi * (((np.arange(K) - K // 2)[:, None] * pixels[None, :]) % height) / height
    scaling = 1.0 / math.sqrt(height * KP)
    fc, fs = np.cos(angles) * scaling, -np.sin(angles) * scaling
    coarse = np.arange(N)
    back = 2.0 * np.pi * ((coarse[:, None] * (np.arange(KP) - KP // 2)[None, :]) % N) / N
    bc, bs = np.cos(back), np.sin(back)
    band = np.arange(1, KP)
    step = height // N
    delta = (pixels[:, None] - step * coarse[None, :]) % height
    up = (1.0 + 2.0 * np.cos(2.0 * np.pi * ((delta[..., None] * band) % height) / height).sum(-1)) / N

    both = np.concatenate([fc, fs], axis=0)
    row_in = np.stack([thrice(both[:, s * rows : (s + 1) * rows]) for s in range(src_devices)])
    col_in = beside(np.concatenate([spaced(fc.T, fs.T), spaced(-fs.T, fc.T)], axis=0))
    half_in = np.zeros((LANES, LANES))
    half_in[:KP] = np.concatenate([bc.T, bs.T], axis=1)
    half_in[HALF : HALF + KP] = np.concatenate([-bs.T, bc.T], axis=1)
    half_in = beside(half_in)
    field_in = thrice(np.concatenate([bc, bs], axis=1))
    up_rows = thrice(up)
    up_cols = beside(np.concatenate([up.T, np.zeros_like(up.T)], axis=0))
    down_cols = beside(np.concatenate([up, up], axis=1))
    down_rows = above(up.T)
    field_back = thrice(np.concatenate([bc.T, bs.T], axis=0))
    half_back = beside(np.concatenate([spaced(bc, -bs), spaced(bs, bc)], axis=0))
    col_back = np.zeros((LANES, 2 * height))
    col_back[:K] = np.concatenate([fc, -fs], axis=1)
    col_back[HALF : HALF + K] = np.concatenate([fs, fc], axis=1)
    col_back = beside(col_back)
    row_back = np.stack([above(both[:, s * rows : (s + 1) * rows].T) for s in range(src_devices)])
    return dict(
        row_in=row_in, col_in=col_in, half_in=half_in, field_in=field_in, up_rows=up_rows, up_cols=up_cols,
        down_cols=down_cols, down_rows=down_rows, field_back=field_back, half_back=half_back,
        col_back=col_back, row_back=row_back,
    )


ORDER = (
    "row_in", "col_in", "half_in", "field_in", "up_rows", "up_cols",
    "down_cols", "down_rows", "field_back", "half_back", "col_back", "row_back",
)
PER_SOURCE = ("row_in", "row_back")


def mm(left, right):
    return jnp.dot(left, right, preferred_element_type=f32)


def split(value):
    high = value.astype(bf16)
    return high, (value - high.astype(f32)).astype(bf16)


def times_table(value, table):
    high, low = split(value)
    width = table.shape[1] // 2
    first = mm(high, table[:, :width]) + mm(high, table[:, width:])
    return first + mm(low, table[:, :width])


def table_times(table, value):
    high, low = split(value)
    height = table.shape[0] // 2
    first = mm(table, high)
    return first[:height] + first[height:] + mm(table[:height], low)


def table_thrice(table, value):
    high, low = split(value)
    return mm(table, jnp.concatenate([high, high, low], axis=0))


def kernel(
    src_devices, clip_devices, scale,
    shifts_hbm, weights_hbm, masks_hbm, pupils_hbm, labels_hbm, *rest,
):
    count = len(ORDER)
    table_hbm = dict(zip(ORDER, rest[:count]))
    mask_out, term_out = rest[count : count + 2]
    tables = dict(zip(ORDER, rest[count + 2 : 2 * count + 2]))
    (
        shifts, weights, masks, pupils, labels, pupil_real, pupil_imag, fields, padded, total,
        spec_slots, power_slots, grad_slots, term_slots,
        local_sems, spec_send, spec_recv, power_send, power_recv,
        grad_send, grad_recv, term_send, term_recv, result, term_result, out_sems,
    ) = rest[2 * count + 2 :]
    me = lax.axis_index("src")
    my_clip = lax.axis_index("clip")

    barrier = pltpu.get_barrier_semaphore()
    for d in range(1, src_devices):
        pl.semaphore_signal(
            barrier, inc=1, device_id={"src": lax.rem(me + d, src_devices)}, device_id_type=pl.DeviceIdType.MESH
        )
    for d in range(1, clip_devices):
        pl.semaphore_signal(
            barrier, inc=1, device_id={"clip": lax.rem(my_clip + d, clip_devices)},
            device_id_type=pl.DeviceIdType.MESH,
        )

    def bring(name):
        source = table_hbm[name]
        if name in PER_SOURCE:
            source = source.at[me]
        return pltpu.make_async_copy(source, tables[name], local_sems.at[ORDER.index(name)])

    copy_masks = pltpu.make_async_copy(masks_hbm, masks, local_sems.at[count])
    copy_pupils = pltpu.make_async_copy(pupils_hbm, pupils, local_sems.at[count + 1])
    copy_labels = pltpu.make_async_copy(labels_hbm, labels, local_sems.at[count + 2])
    copy_shifts = pltpu.make_async_copy(shifts_hbm, shifts, local_sems.at[count + 3])
    copy_weights = pltpu.make_async_copy(weights_hbm, weights, local_sems.at[count + 4])
    copies = {name: bring(name) for name in ORDER}
    copy_masks.start()
    copies["row_in"].start()
    copies["col_in"].start()
    copy_pupils.start()
    copy_shifts.start()
    copy_weights.start()
    for name in ORDER[2:6]:
        copies[name].start()
    copy_labels.start()
    for name in ORDER[6:]:
        copies[name].start()

    def exchange(axis, devices, mine, slots, send, recv):
        sent = []
        for d in range(1, devices):
            copy = pltpu.make_async_remote_copy(
                src_ref=slots.at[mine], dst_ref=slots.at[mine],
                send_sem=send.at[d - 1], recv_sem=recv.at[d - 1],
                device_id={axis: lax.rem(mine + d, devices)}, device_id_type=pl.DeviceIdType.MESH,
            )
            copy.start()
            sent.append(copy)
        return sent

    def arrive(sent):
        for copy in sent:
            copy.wait_recv()

    def add_slots(slots, devices):
        value = slots[0]
        for d in range(1, devices):
            value = value + slots[d]
        return value

    lane = lax.broadcasted_iota(jnp.int32, (1, LANES), 1)
    low_half = lane < HALF
    sign = jnp.where(low_half, -1.0, 1.0).astype(f32)

    def rotate(value):
        return pltpu.roll(value, HALF, 1) * sign

    copy_masks.wait()
    copies["row_in"].wait()
    copies["col_in"].wait()
    height = masks.shape[2]
    colors = range(2)
    spec_sent, power_sent, grad_sent = [], [], []
    for k in colors:
        rows_done = table_thrice(tables["row_in"][...], masks[k])
        stacked = jnp.concatenate([rows_done[:K], rows_done[K:]], axis=1)
        spec_slots[k, me] = times_table(stacked, tables["col_in"][...])
        if k == 0:
            pl.semaphore_wait(barrier, src_devices + clip_devices - 2)
        spec_sent.append(
            exchange("src", src_devices, me, spec_slots.at[k], spec_send.at[k], spec_recv.at[k])
        )

    copy_pupils.wait()
    channels = pupils.shape[0]
    blank = jnp.zeros((KP, HALF - KP), f32)
    for c in range(channels):
        pr, pi = pupils[c, 0], pupils[c, 1]
        pupil_real[c] = jnp.concatenate([pr, blank, pr, blank], axis=1)
        pupil_imag[c] = jnp.concatenate([pi, blank, pi, blank], axis=1)
    padded[...] = jnp.zeros_like(padded)
    copy_shifts.wait()
    copy_weights.wait()
    first = shifts[0, 0]
    second = shifts[0, 1]
    weight = weights[0]
    copies["half_in"].wait()
    copies["field_in"].wait()

    raw = []
    for k in colors:
        arrive(spec_sent[k])
        total[k] = add_slots(spec_slots.at[k], src_devices)
        window = pltpu.roll(total[k, pl.ds(first, KP), :], lax.rem(LANES - second, LANES), 1)
        turned = rotate(window)
        products = [pupil_real[c] * window + pupil_imag[c] * turned for c in range(channels)]
        half = times_table(jnp.concatenate(products, axis=0), tables["half_in"][...])
        half_high, half_low = split(half)
        turn_high, turn_low = split(rotate(half))
        columns = []
        for c in range(channels):
            rows = slice(c * KP, (c + 1) * KP)
            columns.append(
                jnp.concatenate(
                    [half_high[rows], turn_high[rows], half_high[rows], turn_high[rows], half_low[rows], turn_low[rows]],
                    axis=0,
                )
            )
        wide = mm(tables["field_in"][...], jnp.concatenate(columns, axis=1))
        fields[k] = wide
        squares = wide * wide
        summed = squares[:, :LANES]
        for c in range(1, channels):
            summed = summed + squares[:, c * LANES : (c + 1) * LANES]
        power = (summed + pltpu.roll(summed, HALF, 1)) * (1.0 / (channels * src_devices))
        raw.append(power)
        power_slots[k, me] = jnp.where(low_half, power[: N // 2], power[N // 2 :]) * weight
        power_sent.append(
            exchange("src", src_devices, me, power_slots.at[k], power_send.at[k], power_recv.at[k])
        )
    copies["up_rows"].wait()
    copies["up_cols"].wait()
    copy_labels.wait()
    for name in ORDER[6:]:
        copies[name].wait()

    term = jnp.zeros((1, LANES), f32)
    for k in colors:
        arrive(power_sent[k])
        packed = add_slots(power_slots.at[k], src_devices)
        coarse = jnp.concatenate([packed, pltpu.roll(packed, HALF, 1)], axis=0)
        tall = table_thrice(tables["up_rows"][...], coarse)
        thin = []
        for r in range(0, height, CHUNK):
            intensity = times_table(tall[r : r + CHUNK], tables["up_cols"][...])
            level = jnp.tanh((0.5 * steepness) * (intensity - threshold))
            shifted = level + jnp.where(labels[r : r + CHUNK, :] == k + 1, -1.0, 1.0)
            slope = (0.25 * loss_weight * steepness) * shifted * (1.0 - level * level)
            thin.append(times_table(slope, tables["down_cols"][...]))
        slope = table_times(tables["down_rows"][...], jnp.concatenate(thin, axis=0))
        term = term + jnp.sum(slope * raw[k], axis=0, keepdims=True)
        if k == 1:
            term_slots[my_clip] = jnp.broadcast_to(0.5 * jnp.sum(term, axis=1, keepdims=True), (8, LANES))
            term_sent = exchange("clip", clip_devices, my_clip, term_slots, term_send, term_recv)

        slope = slope * (weight * (2.0 / (channels * src_devices)))
        field_grad = fields[k] * jnp.concatenate([slope] * channels, axis=1)
        back = table_thrice(tables["field_back"][...], field_grad)
        pieces = []
        for c in range(channels):
            block = back[:, c * LANES : (c + 1) * LANES]
            pieces.append(block[:KP] - rotate(block[KP:]))
        product_grad = times_table(jnp.concatenate(pieces, axis=0), tables["half_back"][...])
        along = jnp.zeros((KP, LANES), f32)
        across = jnp.zeros((KP, LANES), f32)
        for c in range(channels):
            block = product_grad[c * KP : (c + 1) * KP]
            along = along + pupil_real[c] * block
            across = across + pupil_imag[c] * block
        window_grad = along - rotate(across)
        padded[k, K - KP : K, :] = pltpu.roll(window_grad, second, 1)
        grad_slots[k, me] = padded[k, pl.ds(K - KP - first, K), :]
        grad_sent.append(
            exchange("src", src_devices, me, grad_slots.at[k], grad_send.at[k], grad_recv.at[k])
        )

    leaving = []
    for k in colors:
        arrive(grad_sent[k])
        spread = times_table(add_slots(grad_slots.at[k], src_devices), tables["col_back"][...])
        folded = jnp.concatenate([spread[:, :height], spread[:, height:]], axis=0)
        plane = masks[k]
        pull = (4.0 * binarize) * (1.0 - plane * plane) * plane
        result[k] = table_times(tables["row_back"][...], folded) - pull
        leaving.append(pltpu.make_async_copy(result.at[k], mask_out.at[k], out_sems.at[k]))
        leaving[-1].start()
        if k == 0:
            arrive(term_sent)
            summed = add_slots(term_slots, clip_devices)
            term_result[0] = jnp.sum(jnp.where(lane == 0, summed[:1], 0.0)) * scale
            leaving.append(pltpu.make_async_copy(term_result, term_out, out_sems.at[2]))
            leaving[-1].start()
    for copy in leaving:
        copy.wait()
    for sent in spec_sent + power_sent + [term_sent] + grad_sent:
        for copy in sent:
            copy.wait_send()


def hand_on(mask_in, term_in, mask_out, term_out, sems):
    copies = [
        pltpu.make_async_copy(mask_in, mask_out, sems.at[0]),
        pltpu.make_async_copy(term_in, term_out, sems.at[1]),
    ]
    for copy in copies:
        copy.start()
    for copy in copies:
        copy.wait()


def per_device(color_masks, source_weights, pupil_shifts, pupils, target_labels):
    src_devices = lax.axis_size("src")
    clip_devices = lax.axis_size("clip")
    rows, height = color_masks.shape[2], color_masks.shape[3]
    channels = pupils.shape[0]
    tables = make_tables(height, src_devices)
    masks_here = color_masks[0]
    scale = src_devices / (2.0 * clip_devices * height * height)
    operands = [jnp.asarray(tables[name]) for name in ORDER]
    table_scratch = []
    for name in ORDER:
        shape = tables[name].shape[1:] if name in PER_SOURCE else tables[name].shape
        table_scratch.append(pltpu.VMEM(shape, bf16))
    far = pl.BlockSpec(memory_space=pltpu.HBM)
    dma = pltpu.SemaphoreType.DMA
    mask_grad, terms = pl.pallas_call(
        functools.partial(kernel, src_devices, clip_devices, scale),
        out_shape=(
            jax.ShapeDtypeStruct((2, rows, height), f32),
            jax.ShapeDtypeStruct((1,), f32),
        ),
        in_specs=[far] * (5 + len(ORDER)),
        out_specs=(far, far),
        scratch_shapes=table_scratch
        + [
            pltpu.SMEM((1, 2), jnp.int32),
            pltpu.SMEM((1,), f32),
            pltpu.VMEM((2, rows, height), f32),
            pltpu.VMEM(pupils.shape, f32),
            pltpu.VMEM((height, height), jnp.int32),
            pltpu.VMEM((channels, KP, LANES), f32),
            pltpu.VMEM((channels, KP, LANES), f32),
            pltpu.VMEM((2, N, channels * LANES), f32),
            pltpu.VMEM((2, 2 * K - KP, LANES), f32),
            pltpu.VMEM((2, K, LANES), f32),
            pltpu.VMEM((2, src_devices, K, LANES), f32),
            pltpu.VMEM((2, src_devices, N // 2, LANES), f32),
            pltpu.VMEM((2, src_devices, K, LANES), f32),
            pltpu.VMEM((clip_devices, 8, LANES), f32),
            dma((len(ORDER) + 5,)),
        ]
        + [dma((2, src_devices - 1))] * 6
        + [dma((clip_devices - 1,))] * 2
        + [pltpu.VMEM((2, rows, height), f32), pltpu.SMEM((1,), f32), dma((3,))],
        compiler_params=pltpu.CompilerParams(
            collective_id=0, has_side_effects=True, vmem_limit_bytes=60 * 1024 * 1024
        ),
        name="abbe_gradient",
    )(pupil_shifts, source_weights, masks_here, pupils, target_labels[0], *operands)
    mask_grad, terms = pl.pallas_call(
        hand_on,
        out_shape=(
            jax.ShapeDtypeStruct((2, rows, height), f32),
            jax.ShapeDtypeStruct((1,), f32),
        ),
        in_specs=[far, far],
        out_specs=(far, far),
        scratch_shapes=[dma((2,))],
        compiler_params=pltpu.CompilerParams(vmem_limit_bytes=60 * 1024 * 1024),
        name="hand_on",
    )(mask_grad, terms)
    return mask_grad[None], terms


def solution(mesh):
    in_specs = (P("clip", None, "src", None), P("src"), P("src", None), P(), P("clip", None, None))
    out_specs = (P("clip", None, "src", None), P("src"))
    return jax.shard_map(
        per_device, mesh=mesh, in_specs=in_specs, out_specs=out_specs, check_vma=False
    )
```

```python
import functools
import math

import jax
import jax.numpy as jnp
import ml_dtypes
import numpy as np
from jax import lax
from jax.experimental import pallas as pl
from jax.experimental.pallas import tpu as pltpu
from jax.sharding import PartitionSpec as P

K = 48
KP = 32
N = 2 * KP
LANES = 128
HALF = 64
CHUNK = 64

steepness = 4.0
threshold = 0.6
loss_weight = 2.0
binarize = 0.25
f32 = jnp.float32
bf16 = jnp.bfloat16


def halves(table):
    high = table.astype(np.float32).astype(ml_dtypes.bfloat16)
    low = (table - high.astype(np.float64)).astype(np.float32).astype(ml_dtypes.bfloat16)
    return high, low


def beside(table):
    return np.concatenate(halves(table), axis=-1)


def above(table):
    return np.concatenate(halves(table), axis=-2)


def thrice(table):
    high, low = halves(table)
    return np.concatenate([high, low, high], axis=-1)


def spaced(real, imag):
    out = np.zeros((real.shape[0], LANES))
    out[:, : real.shape[1]] = real
    out[:, HALF : HALF + imag.shape[1]] = imag
    return out


def make_tables(height, src_devices):
    rows = height // src_devices
    pixels = np.arange(height)
    angles = 2.0 * np.pi * (((np.arange(K) - K // 2)[:, None] * pixels[None, :]) % height) / height
    scaling = 1.0 / math.sqrt(height * KP)
    fc, fs = np.cos(angles) * scaling, -np.sin(angles) * scaling
    coarse = np.arange(N)
    back = 2.0 * np.pi * ((coarse[:, None] * (np.arange(KP) - KP // 2)[None, :]) % N) / N
    bc, bs = np.cos(back), np.sin(back)
    band = np.arange(1, KP)
    step = height // N
    delta = (pixels[:, None] - step * coarse[None, :]) % height
    up = (1.0 + 2.0 * np.cos(2.0 * np.pi * ((delta[..., None] * band) % height) / height).sum(-1)) / N

    both = np.concatenate([fc, fs], axis=0)
    row_in = np.stack([thrice(both[:, s * rows : (s + 1) * rows]) for s in range(src_devices)])
    col_in = beside(np.concatenate([spaced(fc.T, fs.T), spaced(-fs.T, fc.T)], axis=0))
    half_in = np.zeros((LANES, LANES))
    half_in[:KP] = np.concatenate([bc.T, bs.T], axis=1)
    half_in[HALF : HALF + KP] = np.concatenate([-bs.T, bc.T], axis=1)
    half_in = beside(half_in)
    field_in = thrice(np.concatenate([bc, bs], axis=1))
    up_rows = thrice(up)
    up_cols = beside(np.concatenate([up.T, np.zeros_like(up.T)], axis=0))
    down_cols = beside(np.concatenate([up, up], axis=1))
    down_rows = above(up.T)
    field_back = thrice(np.concatenate([bc.T, bs.T], axis=0))
    half_back = beside(np.concatenate([spaced(bc, -bs), spaced(bs, bc)], axis=0))
    col_back = np.zeros((LANES, 2 * height))
    col_back[:K] = np.concatenate([fc, -fs], axis=1)
    col_back[HALF : HALF + K] = np.concatenate([fs, fc], axis=1)
    col_back = beside(col_back)
    row_back = np.stack([above(both[:, s * rows : (s + 1) * rows].T) for s in range(src_devices)])
    return dict(
        row_in=row_in, col_in=col_in, half_in=half_in, field_in=field_in, up_rows=up_rows, up_cols=up_cols,
        down_cols=down_cols, down_rows=down_rows, field_back=field_back, half_back=half_back,
        col_back=col_back, row_back=row_back,
    )


ORDER = (
    "row_in", "col_in", "half_in", "field_in", "up_rows", "up_cols",
    "down_cols", "down_rows", "field_back", "half_back", "col_back", "row_back",
)
PER_SOURCE = ("row_in", "row_back")


def mm(left, right):
    return jnp.dot(left, right, preferred_element_type=f32)


def split(value):
    high = value.astype(bf16)
    return high, (value - high.astype(f32)).astype(bf16)


def times_table(value, table):
    high, low = split(value)
    width = table.shape[1] // 2
    first = mm(high, table[:, :width]) + mm(high, table[:, width:])
    return first + mm(low, table[:, :width])


def table_times(table, value):
    high, low = split(value)
    height = table.shape[0] // 2
    first = mm(table, high)
    return first[:height] + first[height:] + mm(table[:height], low)


def table_thrice(table, value):
    high, low = split(value)
    return mm(table, jnp.concatenate([high, high, low], axis=0))


def kernel(
    src_devices, clip_devices, scale,
    shifts_hbm, weights_hbm, masks_hbm, pupils_hbm, labels_hbm, *rest,
):
    count = len(ORDER)
    table_hbm = dict(zip(ORDER, rest[:count]))
    mask_out, term_out = rest[count : count + 2]
    tables = dict(zip(ORDER, rest[count + 2 : 2 * count + 2]))
    (
        shifts, weights, masks, pupils, labels, pupil_real, pupil_imag, fields, padded, total,
        spec_slots, power_slots, grad_slots, term_slots,
        local_sems, spec_send, spec_recv, power_send, power_recv,
        grad_send, grad_recv, term_send, term_recv, result, term_result, out_sems,
    ) = rest[2 * count + 2 :]
    me = lax.axis_index("src")
    my_clip = lax.axis_index("clip")

    def bring(name):
        source = table_hbm[name]
        if name in PER_SOURCE:
            source = source.at[me]
        return pltpu.make_async_copy(source, tables[name], local_sems.at[ORDER.index(name)])

    copy_masks = pltpu.make_async_copy(masks_hbm, masks, local_sems.at[count])
    copy_pupils = pltpu.make_async_copy(pupils_hbm, pupils, local_sems.at[count + 1])
    copy_labels = pltpu.make_async_copy(labels_hbm, labels, local_sems.at[count + 2])
    copy_shifts = pltpu.make_async_copy(shifts_hbm, shifts, local_sems.at[count + 3])
    copy_weights = pltpu.make_async_copy(weights_hbm, weights, local_sems.at[count + 4])
    copies = {name: bring(name) for name in ORDER}
    copy_masks.start()
    copies["row_in"].start()
    copies["col_in"].start()

    barrier = pltpu.get_barrier_semaphore()
    for d in range(1, src_devices):
        pl.semaphore_signal(
            barrier, inc=1, device_id={"src": lax.rem(me + d, src_devices)}, device_id_type=pl.DeviceIdType.MESH
        )
    for d in range(1, clip_devices):
        pl.semaphore_signal(
            barrier, inc=1, device_id={"clip": lax.rem(my_clip + d, clip_devices)},
            device_id_type=pl.DeviceIdType.MESH,
        )

    copy_pupils.start()
    copy_shifts.start()
    copy_weights.start()
    for name in ORDER[2:6]:
        copies[name].start()
    copy_labels.start()
    for name in ORDER[6:]:
        copies[name].start()

    def exchange(axis, devices, mine, slots, send, recv):
        sent = []
        for d in range(1, devices):
            copy = pltpu.make_async_remote_copy(
                src_ref=slots.at[mine], dst_ref=slots.at[mine],
                send_sem=send.at[d - 1], recv_sem=recv.at[d - 1],
                device_id={axis: lax.rem(mine + d, devices)}, device_id_type=pl.DeviceIdType.MESH,
            )
            copy.start()
            sent.append(copy)
        return sent

    def arrive(sent):
        for copy in sent:
            copy.wait_recv()

    def add_slots(slots, devices):
        value = slots[0]
        for d in range(1, devices):
            value = value + slots[d]
        return value

    lane = lax.broadcasted_iota(jnp.int32, (1, LANES), 1)
    low_half = lane < HALF
    sign = jnp.where(low_half, -1.0, 1.0).astype(f32)

    def rotate(value):
        return pltpu.roll(value, HALF, 1) * sign

    copy_masks.wait()
    copies["row_in"].wait()
    copies["col_in"].wait()
    height = masks.shape[2]
    colors = range(2)
    spec_sent, power_sent, grad_sent = [], [], []
    for k in colors:
        rows_done = table_thrice(tables["row_in"][...], masks[k])
        stacked = jnp.concatenate([rows_done[:K], rows_done[K:]], axis=1)
        spec_slots[k, me] = times_table(stacked, tables["col_in"][...])
        if k == 0:
            pl.semaphore_wait(barrier, src_devices + clip_devices - 2)
        spec_sent.append(
            exchange("src", src_devices, me, spec_slots.at[k], spec_send.at[k], spec_recv.at[k])
        )

    copy_pupils.wait()
    channels = pupils.shape[0]
    blank = jnp.zeros((KP, HALF - KP), f32)
    for c in range(channels):
        pr, pi = pupils[c, 0], pupils[c, 1]
        pupil_real[c] = jnp.concatenate([pr, blank, pr, blank], axis=1)
        pupil_imag[c] = jnp.concatenate([pi, blank, pi, blank], axis=1)
    padded[...] = jnp.zeros_like(padded)
    copy_shifts.wait()
    copy_weights.wait()
    first = shifts[0, 0]
    second = shifts[0, 1]
    weight = weights[0]
    copies["half_in"].wait()
    copies["field_in"].wait()

    raw = []
    for k in colors:
        arrive(spec_sent[k])
        total[k] = add_slots(spec_slots.at[k], src_devices)
        window = pltpu.roll(total[k, pl.ds(first, KP), :], lax.rem(LANES - second, LANES), 1)
        turned = rotate(window)
        products = [pupil_real[c] * window + pupil_imag[c] * turned for c in range(channels)]
        half = times_table(jnp.concatenate(products, axis=0), tables["half_in"][...])
        half_high, half_low = split(half)
        turn_high, turn_low = split(rotate(half))
        columns = []
        for c in range(channels):
            rows = slice(c * KP, (c + 1) * KP)
            columns.append(
                jnp.concatenate(
                    [half_high[rows], turn_high[rows], half_high[rows], turn_high[rows], half_low[rows], turn_low[rows]],
                    axis=0,
                )
            )
        wide = mm(tables["field_in"][...], jnp.concatenate(columns, axis=1))
        fields[k] = wide
        squares = wide * wide
        summed = squares[:, :LANES]
        for c in range(1, channels):
            summed = summed + squares[:, c * LANES : (c + 1) * LANES]
        power = (summed + pltpu.roll(summed, HALF, 1)) * (1.0 / (channels * src_devices))
        raw.append(power)
        power_slots[k, me] = jnp.where(low_half, power[: N // 2], power[N // 2 :]) * weight
        power_sent.append(
            exchange("src", src_devices, me, power_slots.at[k], power_send.at[k], power_recv.at[k])
        )
    copies["up_rows"].wait()
    copies["up_cols"].wait()
    copy_labels.wait()
    for name in ORDER[6:]:
        copies[name].wait()

    term = jnp.zeros((1, LANES), f32)
    for k in colors:
        arrive(power_sent[k])
        packed = add_slots(power_slots.at[k], src_devices)
        coarse = jnp.concatenate([packed, pltpu.roll(packed, HALF, 1)], axis=0)
        tall = table_thrice(tables["up_rows"][...], coarse)
        thin = []
        for r in range(0, height, CHUNK):
            intensity = times_table(tall[r : r + CHUNK], tables["up_cols"][...])
            level = jnp.tanh((0.5 * steepness) * (intensity - threshold))
            shifted = level + jnp.where(labels[r : r + CHUNK, :] == k + 1, -1.0, 1.0)
            slope = (0.25 * loss_weight * steepness) * shifted * (1.0 - level * level)
            thin.append(times_table(slope, tables["down_cols"][...]))
        slope = table_times(tables["down_rows"][...], jnp.concatenate(thin, axis=0))
        term = term + jnp.sum(slope * raw[k], axis=0, keepdims=True)
        slope = slope * (weight * (2.0 / (channels * src_devices)))
        field_grad = fields[k] * jnp.concatenate([slope] * channels, axis=1)
        back = table_thrice(tables["field_back"][...], field_grad)
        pieces = []
        for c in range(channels):
            block = back[:, c * LANES : (c + 1) * LANES]
            pieces.append(block[:KP] - rotate(block[KP:]))
        product_grad = times_table(jnp.concatenate(pieces, axis=0), tables["half_back"][...])
        along = jnp.zeros((KP, LANES), f32)
        across = jnp.zeros((KP, LANES), f32)
        for c in range(channels):
            block = product_grad[c * KP : (c + 1) * KP]
            along = along + pupil_real[c] * block
            across = across + pupil_imag[c] * block
        window_grad = along - rotate(across)
        padded[k, K - KP : K, :] = pltpu.roll(window_grad, second, 1)
        grad_slots[k, me] = padded[k, pl.ds(K - KP - first, K), :]
        grad_sent.append(
            exchange("src", src_devices, me, grad_slots.at[k], grad_send.at[k], grad_recv.at[k])
        )

    term_slots[my_clip] = jnp.broadcast_to(0.5 * jnp.sum(term, axis=1, keepdims=True), (8, LANES))
    term_sent = exchange("clip", clip_devices, my_clip, term_slots, term_send, term_recv)

    leaving = []
    for k in colors:
        if k == 1:
            for sent in spec_sent + power_sent + grad_sent[:1] + [term_sent]:
                for copy in sent:
                    copy.wait_send()
        arrive(grad_sent[k])
        spread = times_table(add_slots(grad_slots.at[k], src_devices), tables["col_back"][...])
        folded = jnp.concatenate([spread[:, :height], spread[:, height:]], axis=0)
        plane = masks[k]
        pull = (4.0 * binarize) * (1.0 - plane * plane) * plane
        result[k] = table_times(tables["row_back"][...], folded) - pull
        leaving.append(pltpu.make_async_copy(result.at[k], mask_out.at[k], out_sems.at[k]))
        leaving[-1].start()
        if k == 0:
            arrive(term_sent)
            summed = add_slots(term_slots, clip_devices)
            term_result[0] = jnp.sum(jnp.where(lane == 0, summed[:1], 0.0)) * scale
            leaving.append(pltpu.make_async_copy(term_result, term_out, out_sems.at[2]))
            leaving[-1].start()
    for copy in grad_sent[1]:
        copy.wait_send()
    for copy in leaving:
        copy.wait()


def hand_on(mask_in, term_in, mask_out, term_out, held, term_held, sems):
    colors = range(mask_in.shape[0])
    arriving = [pltpu.make_async_copy(mask_in.at[k], held.at[k], sems.at[k]) for k in colors]
    leaving = [pltpu.make_async_copy(held.at[k], mask_out.at[k], sems.at[2 + k]) for k in colors]
    arriving.append(pltpu.make_async_copy(term_in, term_held, sems.at[4]))
    leaving.append(pltpu.make_async_copy(term_held, term_out, sems.at[5]))
    for copy in arriving:
        copy.start()
    for before, after in zip(arriving, leaving):
        before.wait()
        after.start()
    for copy in leaving:
        copy.wait()


def per_device(color_masks, source_weights, pupil_shifts, pupils, target_labels):
    src_devices = lax.axis_size("src")
    clip_devices = lax.axis_size("clip")
    rows, height = color_masks.shape[2], color_masks.shape[3]
    channels = pupils.shape[0]
    tables = make_tables(height, src_devices)
    masks_here = color_masks[0]
    scale = src_devices / (2.0 * clip_devices * height * height)
    operands = [jnp.asarray(tables[name]) for name in ORDER]
    table_scratch = []
    for name in ORDER:
        shape = tables[name].shape[1:] if name in PER_SOURCE else tables[name].shape
        table_scratch.append(pltpu.VMEM(shape, bf16))
    far = pl.BlockSpec(memory_space=pltpu.HBM)
    dma = pltpu.SemaphoreType.DMA
    mask_grad, terms = pl.pallas_call(
        functools.partial(kernel, src_devices, clip_devices, scale),
        out_shape=(
            jax.ShapeDtypeStruct((2, rows, height), f32),
            jax.ShapeDtypeStruct((1,), f32),
        ),
        in_specs=[far] * (5 + len(ORDER)),
        out_specs=(far, far),
        scratch_shapes=table_scratch
        + [
            pltpu.SMEM((1, 2), jnp.int32),
            pltpu.SMEM((1,), f32),
            pltpu.VMEM((2, rows, height), f32),
            pltpu.VMEM(pupils.shape, f32),
            pltpu.VMEM((height, height), jnp.int32),
            pltpu.VMEM((channels, KP, LANES), f32),
            pltpu.VMEM((channels, KP, LANES), f32),
            pltpu.VMEM((2, N, channels * LANES), f32),
            pltpu.VMEM((2, 2 * K - KP, LANES), f32),
            pltpu.VMEM((2, K, LANES), f32),
            pltpu.VMEM((2, src_devices, K, LANES), f32),
            pltpu.VMEM((2, src_devices, N // 2, LANES), f32),
            pltpu.VMEM((2, src_devices, K, LANES), f32),
            pltpu.VMEM((clip_devices, 8, LANES), f32),
            dma((len(ORDER) + 5,)),
        ]
        + [dma((2, src_devices - 1))] * 6
        + [dma((clip_devices - 1,))] * 2
        + [pltpu.VMEM((2, rows, height), f32), pltpu.SMEM((1,), f32), dma((3,))],
        compiler_params=pltpu.CompilerParams(
            collective_id=0, has_side_effects=True, vmem_limit_bytes=60 * 1024 * 1024
        ),
        name="abbe_gradient",
    )(pupil_shifts, source_weights, masks_here, pupils, target_labels[0], *operands)
    mask_grad, terms = pl.pallas_call(
        hand_on,
        out_shape=(
            jax.ShapeDtypeStruct((2, rows, height), f32),
            jax.ShapeDtypeStruct((1,), f32),
        ),
        in_specs=[far, far],
        out_specs=(far, far),
        scratch_shapes=[pltpu.VMEM((2, rows, height), f32), pltpu.SMEM((1,), f32), dma((6,))],
        compiler_params=pltpu.CompilerParams(vmem_limit_bytes=60 * 1024 * 1024),
        name="hand_on",
    )(mask_grad, terms)
    return mask_grad[None], terms


def solution(mesh):
    in_specs = (P("clip", None, "src", None), P("src"), P("src", None), P(), P("clip", None, None))
    out_specs = (P("clip", None, "src", None), P("src"))
    return jax.shard_map(
        per_device, mesh=mesh, in_specs=in_specs, out_specs=out_specs, check_vma=False
    )
```

```python
import functools
import math

import jax
import jax.numpy as jnp
import ml_dtypes
import numpy as np
from jax import lax
from jax.experimental import pallas as pl
from jax.experimental.pallas import tpu as pltpu
from jax.sharding import PartitionSpec as P

K = 48
KP = 32
N = 2 * KP
LANES = 128
HALF = 64
CHUNK = 64

steepness = 4.0
threshold = 0.6
loss_weight = 2.0
binarize = 0.25
f32 = jnp.float32
bf16 = jnp.bfloat16


def halves(table):
    high = table.astype(np.float32).astype(ml_dtypes.bfloat16)
    low = (table - high.astype(np.float64)).astype(np.float32).astype(ml_dtypes.bfloat16)
    return high, low


def beside(table):
    return np.concatenate(halves(table), axis=-1)


def above(table):
    return np.concatenate(halves(table), axis=-2)


def thrice(table):
    high, low = halves(table)
    return np.concatenate([high, low, high], axis=-1)


def crossed(table):
    high, low = halves(table)
    return np.concatenate(
        [np.concatenate([high, low], axis=1), np.concatenate([high, np.zeros_like(low)], axis=1)], axis=0
    )


def crossed_left(table):
    high, low = halves(table)
    return np.concatenate(
        [np.concatenate([high, high], axis=1), np.concatenate([low, np.zeros_like(low)], axis=1)], axis=0
    )


def spaced(real, imag):
    out = np.zeros((real.shape[0], LANES))
    out[:, : real.shape[1]] = real
    out[:, HALF : HALF + imag.shape[1]] = imag
    return out


def make_tables(height, src_devices):
    rows = height // src_devices
    pixels = np.arange(height)
    angles = 2.0 * np.pi * (((np.arange(K) - K // 2)[:, None] * pixels[None, :]) % height) / height
    scaling = 1.0 / math.sqrt(height * KP)
    fc, fs = np.cos(angles) * scaling, -np.sin(angles) * scaling
    coarse = np.arange(N)
    back = 2.0 * np.pi * ((coarse[:, None] * (np.arange(KP) - KP // 2)[None, :]) % N) / N
    bc, bs = np.cos(back), np.sin(back)
    band = np.arange(1, KP)
    step = height // N
    delta = (pixels[:, None] - step * coarse[None, :]) % height
    up = (1.0 + 2.0 * np.cos(2.0 * np.pi * ((delta[..., None] * band) % height) / height).sum(-1)) / N

    both = np.concatenate([fc, fs], axis=0)
    row_in = np.stack([thrice(both[:, s * rows : (s + 1) * rows]) for s in range(src_devices)])
    col_in = beside(spaced(fc.T, fs.T))
    half_in = np.zeros((LANES, LANES))
    half_in[:KP] = np.concatenate([bc.T, bs.T], axis=1)
    half_in[HALF : HALF + KP] = np.concatenate([-bs.T, bc.T], axis=1)
    half_in = crossed(half_in)
    field_in = thrice(np.concatenate([bc, bs], axis=1))
    up_rows = thrice(up)
    high, low = halves(up.T)
    up_cols = np.concatenate([high, high, low, np.zeros_like(low)], axis=0)
    down_cols = crossed(up)
    down_rows = above(up.T)
    field_back = thrice(np.concatenate([bc.T, bs.T], axis=0))
    half_back = crossed(np.concatenate([spaced(bc, -bs), spaced(bs, bc)], axis=0))
    col_back = np.zeros((LANES, height))
    col_back[:K], col_back[HALF : HALF + K] = fc, fs
    high, low = halves(col_back)
    col_back = np.concatenate([high, high, low], axis=0)
    row_back = np.stack([crossed_left(both[:, s * rows : (s + 1) * rows].T) for s in range(src_devices)])
    return dict(
        row_in=row_in, col_in=col_in, half_in=half_in, field_in=field_in, up_rows=up_rows, up_cols=up_cols,
        down_cols=down_cols, down_rows=down_rows, field_back=field_back, half_back=half_back,
        col_back=col_back, row_back=row_back,
    )


ORDER = (
    "row_in", "col_in", "half_in", "field_in", "up_rows", "up_cols",
    "down_cols", "down_rows", "field_back", "half_back", "col_back", "row_back",
)
PER_SOURCE = ("row_in", "row_back")


def mm(left, right):
    return jnp.dot(left, right, preferred_element_type=f32)


def split(value):
    high = value.astype(bf16)
    return high, (value - high.astype(f32)).astype(bf16)


def add_halves(value):
    width = value.shape[1] // 2
    return value[:, :width] + value[:, width:]


def times_crossed(value, table):
    return mm(jnp.concatenate(split(value), axis=1), table)


def table_thrice(table, value):
    high, low = split(value)
    return mm(table, jnp.concatenate([high, high, low], axis=0))


def kernel(
    src_devices, clip_devices, scale,
    shifts_hbm, weights_hbm, masks_hbm, pupils_hbm, labels_hbm, *rest,
):
    count = len(ORDER)
    table_hbm = dict(zip(ORDER, rest[:count]))
    mask_out, term_out = rest[count : count + 2]
    tables = dict(zip(ORDER, rest[count + 2 : 2 * count + 2]))
    (
        shifts, weights, masks, pupils, labels, pupil_real, pupil_imag, fields, padded, total,
        spec_slots, power_slots, grad_slots, term_slots,
        local_sems, spec_send, spec_recv, power_send, power_recv,
        grad_send, grad_recv, term_send, term_recv, result, term_result, out_sems,
    ) = rest[2 * count + 2 :]
    me = lax.axis_index("src")
    my_clip = lax.axis_index("clip")

    def bring(name):
        source = table_hbm[name]
        if name in PER_SOURCE:
            source = source.at[me]
        return pltpu.make_async_copy(source, tables[name], local_sems.at[ORDER.index(name)])

    copy_masks = pltpu.make_async_copy(masks_hbm, masks, local_sems.at[count])
    copy_pupils = pltpu.make_async_copy(pupils_hbm, pupils, local_sems.at[count + 1])
    copy_labels = pltpu.make_async_copy(labels_hbm, labels, local_sems.at[count + 2])
    copy_shifts = pltpu.make_async_copy(shifts_hbm, shifts, local_sems.at[count + 3])
    copy_weights = pltpu.make_async_copy(weights_hbm, weights, local_sems.at[count + 4])
    copies = {name: bring(name) for name in ORDER}
    copy_masks.start()
    copies["row_in"].start()
    copies["col_in"].start()

    barrier = pltpu.get_barrier_semaphore()
    for d in range(1, src_devices):
        pl.semaphore_signal(
            barrier, inc=1, device_id={"src": lax.rem(me + d, src_devices)}, device_id_type=pl.DeviceIdType.MESH
        )
    for d in range(1, clip_devices):
        pl.semaphore_signal(
            barrier, inc=1, device_id={"clip": lax.rem(my_clip + d, clip_devices)},
            device_id_type=pl.DeviceIdType.MESH,
        )

    copy_pupils.start()
    copy_shifts.start()
    copy_weights.start()
    for name in ORDER[2:6]:
        copies[name].start()
    copy_labels.start()
    for name in ORDER[6:]:
        copies[name].start()

    def exchange(axis, devices, mine, slots, send, recv):
        sent = []
        for d in range(1, devices):
            copy = pltpu.make_async_remote_copy(
                src_ref=slots.at[mine], dst_ref=slots.at[mine],
                send_sem=send.at[d - 1], recv_sem=recv.at[d - 1],
                device_id={axis: lax.rem(mine + d, devices)}, device_id_type=pl.DeviceIdType.MESH,
            )
            copy.start()
            sent.append(copy)
        return sent

    def arrive(sent):
        for copy in sent:
            copy.wait_recv()

    def add_slots(slots, devices):
        value = slots[0]
        for d in range(1, devices):
            value = value + slots[d]
        return value

    lane = lax.broadcasted_iota(jnp.int32, (1, LANES), 1)
    low_half = lane < HALF
    sign = jnp.where(low_half, -1.0, 1.0).astype(f32)

    def rotate(value):
        return pltpu.roll(value, HALF, 1) * sign

    copy_masks.wait()
    copies["row_in"].wait()
    copies["col_in"].wait()
    height = masks.shape[2]
    colors = range(2)
    spec_sent, power_sent, grad_sent = [], [], []
    for k in colors:
        rows_done = table_thrice(tables["row_in"][...], masks[k])
        pair = mm(jnp.concatenate(split(rows_done), axis=0), tables["col_in"][...])
        done = pair[: 2 * K, :LANES] + pair[: 2 * K, LANES:] + pair[2 * K :, :LANES]
        spec_slots[k, me] = done[:K] + rotate(done[K:])
        if k == 0:
            pl.semaphore_wait(barrier, src_devices + clip_devices - 2)
        spec_sent.append(
            exchange("src", src_devices, me, spec_slots.at[k], spec_send.at[k], spec_recv.at[k])
        )

    copy_pupils.wait()
    channels = pupils.shape[0]
    blank = jnp.zeros((KP, HALF - KP), f32)
    for c in range(channels):
        pr, pi = pupils[c, 0], pupils[c, 1]
        pupil_real[c] = jnp.concatenate([pr, blank, pr, blank], axis=1)
        pupil_imag[c] = jnp.concatenate([pi, blank, pi, blank], axis=1)
    padded[...] = jnp.zeros_like(padded)
    copy_shifts.wait()
    copy_weights.wait()
    first = shifts[0, 0]
    second = shifts[0, 1]
    weight = weights[0]
    copies["half_in"].wait()
    copies["field_in"].wait()

    raw = []
    for k in colors:
        arrive(spec_sent[k])
        total[k] = add_slots(spec_slots.at[k], src_devices)
        window = pltpu.roll(total[k, pl.ds(first, KP), :], lax.rem(LANES - second, LANES), 1)
        turned = rotate(window)
        products = [pupil_real[c] * window + pupil_imag[c] * turned for c in range(channels)]
        half = add_halves(times_crossed(jnp.concatenate(products, axis=0), tables["half_in"][...]))
        half_high, half_low = split(half)
        turn_high, turn_low = split(rotate(half))
        columns = []
        for c in range(channels):
            rows = slice(c * KP, (c + 1) * KP)
            columns.append(
                jnp.concatenate(
                    [half_high[rows], turn_high[rows], half_high[rows], turn_high[rows], half_low[rows], turn_low[rows]],
                    axis=0,
                )
            )
        wide = mm(tables["field_in"][...], jnp.concatenate(columns, axis=1))
        fields[k] = wide
        squares = wide * wide
        summed = squares[:, :LANES]
        for c in range(1, channels):
            summed = summed + squares[:, c * LANES : (c + 1) * LANES]
        power = (summed + pltpu.roll(summed, HALF, 1)) * (1.0 / (channels * src_devices))
        raw.append(power)
        power_slots[k, me] = jnp.where(low_half, power[: N // 2], power[N // 2 :]) * weight
        power_sent.append(
            exchange("src", src_devices, me, power_slots.at[k], power_send.at[k], power_recv.at[k])
        )
    copies["up_rows"].wait()
    copies["up_cols"].wait()
    copy_labels.wait()
    for name in ORDER[6:]:
        copies[name].wait()

    term = jnp.zeros((1, LANES), f32)
    for k in colors:
        arrive(power_sent[k])
        packed = add_slots(power_slots.at[k], src_devices)
        turned = pltpu.roll(packed, HALF, 1)
        coarse = jnp.concatenate(
            [jnp.where(low_half, packed, turned), jnp.where(low_half, turned, packed)], axis=0
        )
        tall = table_thrice(tables["up_rows"][...], coarse)
        thin = []
        for r in range(0, height, CHUNK):
            part = tall[r : r + CHUNK]
            high = part.astype(bf16)
            wide_high = high.astype(f32)
            mixed = jnp.where(low_half, wide_high, part - wide_high).astype(bf16)
            intensity = mm(jnp.concatenate([mixed, high], axis=1), tables["up_cols"][...])
            level = jnp.tanh((0.5 * steepness) * (intensity - threshold))
            shifted = level + jnp.where(labels[r : r + CHUNK, :] == k + 1, -1.0, 1.0)
            slope = (0.25 * loss_weight * steepness) * shifted * (1.0 - level * level)
            thin.append(times_crossed(slope, tables["down_cols"][...]))
        thin = jnp.concatenate(split(jnp.concatenate(thin, axis=0)), axis=1)
        pair = mm(tables["down_rows"][...], thin)
        slope = pair[:N, :LANES] + pair[N:, :LANES] + pair[:N, LANES:]
        slope = slope + pltpu.roll(slope, HALF, 1)
        term = term + jnp.sum(slope * raw[k], axis=0, keepdims=True)
        slope = slope * (weight * (2.0 / (channels * src_devices)))
        field_grad = fields[k] * jnp.concatenate([slope] * channels, axis=1)
        back = table_thrice(tables["field_back"][...], field_grad)
        pieces = []
        for c in range(channels):
            block = back[:, c * LANES : (c + 1) * LANES]
            pieces.append(block[:KP] - rotate(block[KP:]))
        product_grad = add_halves(times_crossed(jnp.concatenate(pieces, axis=0), tables["half_back"][...]))
        along = jnp.zeros((KP, LANES), f32)
        across = jnp.zeros((KP, LANES), f32)
        for c in range(channels):
            block = product_grad[c * KP : (c + 1) * KP]
            along = along + pupil_real[c] * block
            across = across + pupil_imag[c] * block
        window_grad = along - rotate(across)
        padded[k, K - KP : K, :] = pltpu.roll(window_grad, second, 1)
        grad_slots[k, me] = padded[k, pl.ds(K - KP - first, K), :]
        grad_sent.append(
            exchange("src", src_devices, me, grad_slots.at[k], grad_send.at[k], grad_recv.at[k])
        )

    term_slots[my_clip] = jnp.broadcast_to(0.5 * jnp.sum(term, axis=1, keepdims=True), (8, LANES))
    term_sent = exchange("clip", clip_devices, my_clip, term_slots, term_send, term_recv)

    leaving = []
    for k in colors:
        if k == 1:
            for sent in spec_sent + power_sent + grad_sent[:1] + [term_sent]:
                for copy in sent:
                    copy.wait_send()
        arrive(grad_sent[k])
        gathered = add_slots(grad_slots.at[k], src_devices)
        high, low = split(jnp.concatenate([gathered, -rotate(gathered)], axis=0))
        folded = mm(jnp.concatenate([high, low, high], axis=1), tables["col_back"][...])
        pair = mm(tables["row_back"][...], jnp.concatenate(split(folded), axis=0))
        plane = masks[k]
        pull = (4.0 * binarize) * (1.0 - plane * plane) * plane
        result[k] = pair[: result.shape[1]] + pair[result.shape[1] :] - pull
        leaving.append(pltpu.make_async_copy(result.at[k], mask_out.at[k], out_sems.at[k]))
        leaving[-1].start()
        if k == 0:
            arrive(term_sent)
            summed = add_slots(term_slots, clip_devices)
            term_result[0] = jnp.sum(jnp.where(lane == 0, summed[:1], 0.0)) * scale
            leaving.append(pltpu.make_async_copy(term_result, term_out, out_sems.at[2]))
            leaving[-1].start()
    for copy in grad_sent[1]:
        copy.wait_send()
    for copy in leaving:
        copy.wait()


def hand_on(mask_in, term_in, mask_out, term_out, held, term_held, sems):
    colors = range(mask_in.shape[0])
    arriving = [pltpu.make_async_copy(mask_in.at[k], held.at[k], sems.at[k]) for k in colors]
    leaving = [pltpu.make_async_copy(held.at[k], mask_out.at[k], sems.at[2 + k]) for k in colors]
    arriving.append(pltpu.make_async_copy(term_in, term_held, sems.at[4]))
    leaving.append(pltpu.make_async_copy(term_held, term_out, sems.at[5]))
    for copy in arriving:
        copy.start()
    for before, after in zip(arriving, leaving):
        before.wait()
        after.start()
    for copy in leaving:
        copy.wait()


def per_device(color_masks, source_weights, pupil_shifts, pupils, target_labels):
    src_devices = lax.axis_size("src")
    clip_devices = lax.axis_size("clip")
    rows, height = color_masks.shape[2], color_masks.shape[3]
    channels = pupils.shape[0]
    tables = make_tables(height, src_devices)
    masks_here = color_masks[0]
    scale = src_devices / (2.0 * clip_devices * height * height)
    operands = [jnp.asarray(tables[name]) for name in ORDER]
    table_scratch = []
    for name in ORDER:
        shape = tables[name].shape[1:] if name in PER_SOURCE else tables[name].shape
        table_scratch.append(pltpu.VMEM(shape, bf16))
    far = pl.BlockSpec(memory_space=pltpu.HBM)
    dma = pltpu.SemaphoreType.DMA
    mask_grad, terms = pl.pallas_call(
        functools.partial(kernel, src_devices, clip_devices, scale),
        out_shape=(
            jax.ShapeDtypeStruct((2, rows, height), f32),
            jax.ShapeDtypeStruct((1,), f32),
        ),
        in_specs=[far] * (5 + len(ORDER)),
        out_specs=(far, far),
        scratch_shapes=table_scratch
        + [
            pltpu.SMEM((1, 2), jnp.int32),
            pltpu.SMEM((1,), f32),
            pltpu.VMEM((2, rows, height), f32),
            pltpu.VMEM(pupils.shape, f32),
            pltpu.VMEM((height, height), jnp.int32),
            pltpu.VMEM((channels, KP, LANES), f32),
            pltpu.VMEM((channels, KP, LANES), f32),
            pltpu.VMEM((2, N, channels * LANES), f32),
            pltpu.VMEM((2, 2 * K - KP, LANES), f32),
            pltpu.VMEM((2, K, LANES), f32),
            pltpu.VMEM((2, src_devices, K, LANES), f32),
            pltpu.VMEM((2, src_devices, N // 2, LANES), f32),
            pltpu.VMEM((2, src_devices, K, LANES), f32),
            pltpu.VMEM((clip_devices, 8, LANES), f32),
            dma((len(ORDER) + 5,)),
        ]
        + [dma((2, src_devices - 1))] * 6
        + [dma((clip_devices - 1,))] * 2
        + [pltpu.VMEM((2, rows, height), f32), pltpu.SMEM((1,), f32), dma((3,))],
        compiler_params=pltpu.CompilerParams(
            collective_id=0, has_side_effects=True, vmem_limit_bytes=60 * 1024 * 1024
        ),
        name="abbe_gradient",
    )(pupil_shifts, source_weights, masks_here, pupils, target_labels[0], *operands)
    mask_grad, terms = pl.pallas_call(
        hand_on,
        out_shape=(
            jax.ShapeDtypeStruct((2, rows, height), f32),
            jax.ShapeDtypeStruct((1,), f32),
        ),
        in_specs=[far, far],
        out_specs=(far, far),
        scratch_shapes=[pltpu.VMEM((2, rows, height), f32), pltpu.SMEM((1,), f32), dma((6,))],
        compiler_params=pltpu.CompilerParams(vmem_limit_bytes=60 * 1024 * 1024),
        name="hand_on",
    )(mask_grad, terms)
    return mask_grad[None], terms


def solution(mesh):
    in_specs = (P("clip", None, "src", None), P("src"), P("src", None), P(), P("clip", None, None))
    out_specs = (P("clip", None, "src", None), P("src"))
    return jax.shard_map(
        per_device, mesh=mesh, in_specs=in_specs, out_specs=out_specs, check_vma=False
    )
```

```python
import functools
import math

import jax
import jax.numpy as jnp
import ml_dtypes
import numpy as np
from jax import lax
from jax.experimental import pallas as pl
from jax.experimental.pallas import tpu as pltpu
from jax.sharding import PartitionSpec as P

K = 48
KP = 32
N = 2 * KP
LANES = 128
HALF = 64
CHUNK = 64

steepness = 4.0
threshold = 0.6
loss_weight = 2.0
binarize = 0.25
f32 = jnp.float32
bf16 = jnp.bfloat16


def halves(table):
    high = table.astype(np.float32).astype(ml_dtypes.bfloat16)
    low = (table - high.astype(np.float64)).astype(np.float32).astype(ml_dtypes.bfloat16)
    return high, low


def beside(table):
    return np.concatenate(halves(table), axis=-1)


def above(table):
    return np.concatenate(halves(table), axis=-2)


def thrice(table):
    high, low = halves(table)
    return np.concatenate([high, low, high], axis=-1)


def crossed(table):
    high, low = halves(table)
    return np.concatenate(
        [np.concatenate([high, low], axis=1), np.concatenate([high, np.zeros_like(low)], axis=1)], axis=0
    )


def crossed_left(table):
    high, low = halves(table)
    return np.concatenate(
        [np.concatenate([high, high], axis=1), np.concatenate([low, np.zeros_like(low)], axis=1)], axis=0
    )


def spaced(real, imag):
    out = np.zeros((real.shape[0], LANES))
    out[:, : real.shape[1]] = real
    out[:, HALF : HALF + imag.shape[1]] = imag
    return out


def make_tables(height, src_devices):
    rows = height // src_devices
    pixels = np.arange(height)
    angles = 2.0 * np.pi * (((np.arange(K) - K // 2)[:, None] * pixels[None, :]) % height) / height
    scaling = 1.0 / math.sqrt(height * KP)
    fc, fs = np.cos(angles) * scaling, -np.sin(angles) * scaling
    coarse = np.arange(N)
    back = 2.0 * np.pi * ((coarse[:, None] * (np.arange(KP) - KP // 2)[None, :]) % N) / N
    bc, bs = np.cos(back), np.sin(back)
    band = np.arange(1, KP)
    step = height // N
    delta = (pixels[:, None] - step * coarse[None, :]) % height
    up = (1.0 + 2.0 * np.cos(2.0 * np.pi * ((delta[..., None] * band) % height) / height).sum(-1)) / N

    both = np.concatenate([fc, fs], axis=0)
    row_in = np.stack([thrice(both[:, s * rows : (s + 1) * rows]) for s in range(src_devices)])
    col_in = beside(spaced(fc.T, fs.T))
    half_in = np.zeros((LANES, LANES))
    half_in[:KP] = np.concatenate([bc.T, bs.T], axis=1)
    half_in[HALF : HALF + KP] = np.concatenate([-bs.T, bc.T], axis=1)
    half_in = crossed(half_in)
    field_in = thrice(np.concatenate([bc, bs], axis=1))
    up_rows = thrice(up)
    high, low = halves(up.T)
    up_cols = np.concatenate([high, high, low, np.zeros_like(low)], axis=0)
    down_cols = crossed(up)
    down_rows = above(up.T)
    field_back = thrice(np.concatenate([bc.T, bs.T], axis=0))
    half_back = crossed(np.concatenate([spaced(bc, -bs), spaced(bs, bc)], axis=0))
    col_back = np.zeros((LANES, height))
    col_back[:K], col_back[HALF : HALF + K] = fc, fs
    high, low = halves(col_back)
    col_back = np.concatenate([high, high, low], axis=0)
    row_back = np.stack([crossed_left(both[:, s * rows : (s + 1) * rows].T) for s in range(src_devices)])
    return dict(
        row_in=row_in, col_in=col_in, half_in=half_in, field_in=field_in, up_rows=up_rows, up_cols=up_cols,
        down_cols=down_cols, down_rows=down_rows, field_back=field_back, half_back=half_back,
        col_back=col_back, row_back=row_back,
    )


ORDER = (
    "row_in", "col_in", "half_in", "field_in", "up_rows", "up_cols",
    "down_cols", "down_rows", "field_back", "half_back", "col_back", "row_back",
)
PER_SOURCE = ("row_in", "row_back")


def mm(left, right):
    return jnp.dot(left, right, preferred_element_type=f32)


def split(value):
    high = value.astype(bf16)
    return high, (value - high.astype(f32)).astype(bf16)


def add_halves(value):
    width = value.shape[1] // 2
    return value[:, :width] + value[:, width:]


def times_crossed(value, table):
    return mm(jnp.concatenate(split(value), axis=1), table)


def table_thrice(table, value):
    high, low = split(value)
    return mm(table, jnp.concatenate([high, high, low], axis=0))


def kernel(
    src_devices, clip_devices, scale,
    shifts_hbm, weights_hbm, masks_hbm, pupils_hbm, labels_hbm, *rest,
):
    count = len(ORDER)
    table_hbm = dict(zip(ORDER, rest[:count]))
    mask_out, term_out = rest[count : count + 2]
    tables = dict(zip(ORDER, rest[count + 2 : 2 * count + 2]))
    (
        shifts, weights, masks, pupils, labels, pupil_real, pupil_imag, fields, padded, total,
        spec_slots, shift_slots, weight_slots, shift_words, term_slots,
        local_sems, spec_send, spec_recv, small_send, small_recv,
        term_send, term_recv, result, term_result, out_sems,
    ) = rest[2 * count + 2 :]
    me = lax.axis_index("src")
    my_clip = lax.axis_index("clip")

    def bring(name):
        source = table_hbm[name]
        if name in PER_SOURCE:
            source = source.at[me]
        return pltpu.make_async_copy(source, tables[name], local_sems.at[ORDER.index(name)])

    copy_masks = pltpu.make_async_copy(masks_hbm, masks, local_sems.at[count])
    copy_pupils = pltpu.make_async_copy(pupils_hbm, pupils, local_sems.at[count + 1])
    copy_labels = pltpu.make_async_copy(labels_hbm, labels, local_sems.at[count + 2])
    copy_shifts = pltpu.make_async_copy(shifts_hbm, shifts, local_sems.at[count + 3])
    copy_weights = pltpu.make_async_copy(weights_hbm, weights, local_sems.at[count + 4])
    copies = {name: bring(name) for name in ORDER}
    copy_masks.start()
    copies["row_in"].start()
    copies["col_in"].start()

    barrier = pltpu.get_barrier_semaphore()
    for d in range(1, src_devices):
        pl.semaphore_signal(
            barrier, inc=1, device_id={"src": lax.rem(me + d, src_devices)}, device_id_type=pl.DeviceIdType.MESH
        )
    for d in range(1, clip_devices):
        pl.semaphore_signal(
            barrier, inc=1, device_id={"clip": lax.rem(my_clip + d, clip_devices)},
            device_id_type=pl.DeviceIdType.MESH,
        )

    copy_pupils.start()
    copy_shifts.start()
    copy_weights.start()
    for name in ORDER[2:6]:
        copies[name].start()
    copy_labels.start()
    for name in ORDER[6:]:
        copies[name].start()

    def exchange(axis, devices, mine, slots, send, recv):
        sent = []
        for d in range(1, devices):
            copy = pltpu.make_async_remote_copy(
                src_ref=slots.at[mine], dst_ref=slots.at[mine],
                send_sem=send.at[d - 1], recv_sem=recv.at[d - 1],
                device_id={axis: lax.rem(mine + d, devices)}, device_id_type=pl.DeviceIdType.MESH,
            )
            copy.start()
            sent.append(copy)
        return sent

    def arrive(sent):
        for copy in sent:
            copy.wait_recv()

    def add_slots(slots, devices):
        value = slots[0]
        for d in range(1, devices):
            value = value + slots[d]
        return value

    lane = lax.broadcasted_iota(jnp.int32, (1, LANES), 1)
    low_half = lane < HALF
    sign = jnp.where(low_half, -1.0, 1.0).astype(f32)

    def rotate(value):
        return pltpu.roll(value, HALF, 1) * sign

    copy_shifts.wait()
    copy_weights.wait()
    shift_slots[me] = jnp.broadcast_to(jnp.where(lane == 0, shifts[0, 0], shifts[0, 1]), (8, LANES))
    weight_slots[me] = jnp.full((8, LANES), weights[0], f32)

    copy_masks.wait()
    copies["row_in"].wait()
    copies["col_in"].wait()
    height = masks.shape[2]
    colors = range(2)
    sources = range(src_devices)
    spec_sent, small_sent = [], []
    for k in colors:
        rows_done = table_thrice(tables["row_in"][...], masks[k])
        pair = mm(jnp.concatenate(split(rows_done), axis=0), tables["col_in"][...])
        done = pair[: 2 * K, :LANES] + pair[: 2 * K, LANES:] + pair[2 * K :, :LANES]
        spec_slots[k, me] = done[:K] + rotate(done[K:])
        if k == 0:
            pl.semaphore_wait(barrier, src_devices + clip_devices - 2)
        spec_sent.append(
            exchange("src", src_devices, me, spec_slots.at[k], spec_send.at[k], spec_recv.at[k])
        )
        if k == 0:
            small_sent = exchange("src", src_devices, me, shift_slots, small_send.at[0], small_recv.at[0])
            small_sent += exchange("src", src_devices, me, weight_slots, small_send.at[1], small_recv.at[1])

    copy_pupils.wait()
    channels = pupils.shape[0]
    blank = jnp.zeros((KP, HALF - KP), f32)
    for c in range(channels):
        pr, pi = pupils[c, 0], pupils[c, 1]
        pupil_real[c] = jnp.concatenate([pr, blank, pr, blank], axis=1)
        pupil_imag[c] = jnp.concatenate([pi, blank, pi, blank], axis=1)
    padded[...] = jnp.zeros_like(padded)
    arrive(small_sent)
    copy_words = pltpu.make_async_copy(shift_slots, shift_words, local_sems.at[count + 5])
    copy_words.start()
    copies["half_in"].wait()
    copies["field_in"].wait()
    copy_words.wait()
    first = [shift_words[s, 0, 0] for s in sources]
    second = [shift_words[s, 0, 1] for s in sources]
    weight = [weight_slots[s, 0:1, :] for s in sources]

    coarse, own = [], []
    for k in colors:
        arrive(spec_sent[k])
        total[k] = add_slots(spec_slots.at[k], src_devices)
        summed_power = jnp.zeros((N, LANES), f32)
        own_power = jnp.zeros((N, LANES), f32)
        for s in sources:
            window = pltpu.roll(total[k, pl.ds(first[s], KP), :], lax.rem(LANES - second[s], LANES), 1)
            turned = rotate(window)
            products = [pupil_real[c] * window + pupil_imag[c] * turned for c in range(channels)]
            half = add_halves(times_crossed(jnp.concatenate(products, axis=0), tables["half_in"][...]))
            half_high, half_low = split(half)
            turn_high, turn_low = split(rotate(half))
            columns = []
            for c in range(channels):
                rows = slice(c * KP, (c + 1) * KP)
                columns.append(
                    jnp.concatenate(
                        [half_high[rows], turn_high[rows], half_high[rows], turn_high[rows], half_low[rows], turn_low[rows]],
                        axis=0,
                    )
                )
            wide = mm(tables["field_in"][...], jnp.concatenate(columns, axis=1))
            fields[k, s] = wide
            squares = wide * wide
            summed = squares[:, :LANES]
            for c in range(1, channels):
                summed = summed + squares[:, c * LANES : (c + 1) * LANES]
            power = (summed + pltpu.roll(summed, HALF, 1)) * (1.0 / (channels * src_devices))
            summed_power = summed_power + power * weight[s]
            own_power = own_power + jnp.where(me == s, power, 0.0)
        coarse.append(summed_power)
        own.append(own_power)
    copies["up_rows"].wait()
    copies["up_cols"].wait()
    copy_labels.wait()
    for name in ORDER[6:]:
        copies[name].wait()

    term = jnp.zeros((1, LANES), f32)
    slopes = []
    for k in colors:
        tall = table_thrice(tables["up_rows"][...], coarse[k])
        thin = []
        for r in range(0, height, CHUNK):
            part = tall[r : r + CHUNK]
            high = part.astype(bf16)
            wide_high = high.astype(f32)
            mixed = jnp.where(low_half, wide_high, part - wide_high).astype(bf16)
            intensity = mm(jnp.concatenate([mixed, high], axis=1), tables["up_cols"][...])
            level = jnp.tanh((0.5 * steepness) * (intensity - threshold))
            shifted = level + jnp.where(labels[r : r + CHUNK, :] == k + 1, -1.0, 1.0)
            slope = (0.25 * loss_weight * steepness) * shifted * (1.0 - level * level)
            thin.append(times_crossed(slope, tables["down_cols"][...]))
        thin = jnp.concatenate(split(jnp.concatenate(thin, axis=0)), axis=1)
        pair = mm(tables["down_rows"][...], thin)
        slope = pair[:N, :LANES] + pair[N:, :LANES] + pair[:N, LANES:]
        slope = slope + pltpu.roll(slope, HALF, 1)
        term = term + jnp.sum(slope * own[k], axis=0, keepdims=True)
        slopes.append(slope)
    term_slots[my_clip] = jnp.broadcast_to(0.5 * jnp.sum(term, axis=1, keepdims=True), (8, LANES))
    term_sent = exchange("clip", clip_devices, my_clip, term_slots, term_send, term_recv)

    leaving = []
    for k in colors:
        gathered = jnp.zeros((K, LANES), f32)
        for s in sources:
            slope = slopes[k] * (weight[s] * (2.0 / (channels * src_devices)))
            field_grad = fields[k, s] * jnp.concatenate([slope] * channels, axis=1)
            back = table_thrice(tables["field_back"][...], field_grad)
            pieces = []
            for c in range(channels):
                block = back[:, c * LANES : (c + 1) * LANES]
                pieces.append(block[:KP] - rotate(block[KP:]))
            product_grad = add_halves(times_crossed(jnp.concatenate(pieces, axis=0), tables["half_back"][...]))
            along = jnp.zeros((KP, LANES), f32)
            across = jnp.zeros((KP, LANES), f32)
            for c in range(channels):
                block = product_grad[c * KP : (c + 1) * KP]
                along = along + pupil_real[c] * block
                across = across + pupil_imag[c] * block
            window_grad = along - rotate(across)
            padded[k, s, K - KP : K, :] = pltpu.roll(window_grad, second[s], 1)
            gathered = gathered + padded[k, s, pl.ds(K - KP - first[s], K), :]

        high, low = split(jnp.concatenate([gathered, -rotate(gathered)], axis=0))
        folded = mm(jnp.concatenate([high, low, high], axis=1), tables["col_back"][...])
        pair = mm(tables["row_back"][...], jnp.concatenate(split(folded), axis=0))
        plane = masks[k]
        pull = (4.0 * binarize) * (1.0 - plane * plane) * plane
        result[k] = pair[: result.shape[1]] + pair[result.shape[1] :] - pull
        leaving.append(pltpu.make_async_copy(result.at[k], mask_out.at[k], out_sems.at[k]))
        leaving[-1].start()
        if k == 0:
            arrive(term_sent)
            summed = add_slots(term_slots, clip_devices)
            term_result[0] = jnp.sum(jnp.where(lane == 0, summed[:1], 0.0)) * scale
            leaving.append(pltpu.make_async_copy(term_result, term_out, out_sems.at[2]))
            leaving[-1].start()
            for sent in spec_sent + [small_sent, term_sent]:
                for copy in sent:
                    copy.wait_send()
    for copy in leaving:
        copy.wait()


def hand_on(mask_in, term_in, mask_out, term_out, held, term_held, sems):
    colors = range(mask_in.shape[0])
    arriving = [pltpu.make_async_copy(mask_in.at[k], held.at[k], sems.at[k]) for k in colors]
    leaving = [pltpu.make_async_copy(held.at[k], mask_out.at[k], sems.at[2 + k]) for k in colors]
    arriving.append(pltpu.make_async_copy(term_in, term_held, sems.at[4]))
    leaving.append(pltpu.make_async_copy(term_held, term_out, sems.at[5]))
    for copy in arriving:
        copy.start()
    for before, after in zip(arriving, leaving):
        before.wait()
        after.start()
    for copy in leaving:
        copy.wait()


def per_device(color_masks, source_weights, pupil_shifts, pupils, target_labels):
    src_devices = lax.axis_size("src")
    clip_devices = lax.axis_size("clip")
    rows, height = color_masks.shape[2], color_masks.shape[3]
    channels = pupils.shape[0]
    tables = make_tables(height, src_devices)
    masks_here = color_masks[0]
    scale = src_devices / (2.0 * clip_devices * height * height)
    operands = [jnp.asarray(tables[name]) for name in ORDER]
    table_scratch = []
    for name in ORDER:
        shape = tables[name].shape[1:] if name in PER_SOURCE else tables[name].shape
        table_scratch.append(pltpu.VMEM(shape, bf16))
    far = pl.BlockSpec(memory_space=pltpu.HBM)
    dma = pltpu.SemaphoreType.DMA
    mask_grad, terms = pl.pallas_call(
        functools.partial(kernel, src_devices, clip_devices, scale),
        out_shape=(
            jax.ShapeDtypeStruct((2, rows, height), f32),
            jax.ShapeDtypeStruct((1,), f32),
        ),
        in_specs=[far] * (5 + len(ORDER)),
        out_specs=(far, far),
        scratch_shapes=table_scratch
        + [
            pltpu.SMEM((1, 2), jnp.int32),
            pltpu.SMEM((1,), f32),
            pltpu.VMEM((2, rows, height), f32),
            pltpu.VMEM(pupils.shape, f32),
            pltpu.VMEM((height, height), jnp.int32),
            pltpu.VMEM((channels, KP, LANES), f32),
            pltpu.VMEM((channels, KP, LANES), f32),
            pltpu.VMEM((2, src_devices, N, channels * LANES), f32),
            pltpu.VMEM((2, src_devices, 2 * K - KP, LANES), f32),
            pltpu.VMEM((2, K, LANES), f32),
            pltpu.VMEM((2, src_devices, K, LANES), f32),
            pltpu.VMEM((src_devices, 8, LANES), jnp.int32),
            pltpu.VMEM((src_devices, 8, LANES), f32),
            pltpu.SMEM((src_devices, 8, LANES), jnp.int32),
            pltpu.VMEM((clip_devices, 8, LANES), f32),
            dma((len(ORDER) + 6,)),
        ]
        + [dma((2, src_devices - 1))] * 4
        + [dma((clip_devices - 1,))] * 2
        + [pltpu.VMEM((2, rows, height), f32), pltpu.SMEM((1,), f32), dma((3,))],
        compiler_params=pltpu.CompilerParams(
            collective_id=0, has_side_effects=True, vmem_limit_bytes=60 * 1024 * 1024
        ),
        name="abbe_gradient",
    )(pupil_shifts, source_weights, masks_here, pupils, target_labels[0], *operands)
    mask_grad, terms = pl.pallas_call(
        hand_on,
        out_shape=(
            jax.ShapeDtypeStruct((2, rows, height), f32),
            jax.ShapeDtypeStruct((1,), f32),
        ),
        in_specs=[far, far],
        out_specs=(far, far),
        scratch_shapes=[pltpu.VMEM((2, rows, height), f32), pltpu.SMEM((1,), f32), dma((6,))],
        compiler_params=pltpu.CompilerParams(vmem_limit_bytes=60 * 1024 * 1024),
        name="hand_on",
    )(mask_grad, terms)
    return mask_grad[None], terms


def solution(mesh):
    in_specs = (P("clip", None, "src", None), P("src"), P("src", None), P(), P("clip", None, None))
    out_specs = (P("clip", None, "src", None), P("src"))
    return jax.shard_map(
        per_device, mesh=mesh, in_specs=in_specs, out_specs=out_specs, check_vma=False
    )
```

```python
import functools
import math

import jax
import jax.numpy as jnp
import ml_dtypes
import numpy as np
from jax import lax
from jax.experimental import pallas as pl
from jax.experimental.pallas import tpu as pltpu
from jax.sharding import PartitionSpec as P

K = 48
KP = 32
N = 2 * KP
LANES = 128
HALF = 64
CHUNK = 64

steepness = 4.0
threshold = 0.6
loss_weight = 2.0
binarize = 0.25
f32 = jnp.float32
bf16 = jnp.bfloat16


def halves(table):
    high = table.astype(np.float32).astype(ml_dtypes.bfloat16)
    low = (table - high.astype(np.float64)).astype(np.float32).astype(ml_dtypes.bfloat16)
    return high, low


def beside(table):
    return np.concatenate(halves(table), axis=-1)


def above(table):
    return np.concatenate(halves(table), axis=-2)


def thrice(table):
    high, low = halves(table)
    return np.concatenate([high, low, high], axis=-1)


def crossed(table):
    high, low = halves(table)
    return np.concatenate(
        [np.concatenate([high, low], axis=1), np.concatenate([high, np.zeros_like(low)], axis=1)], axis=0
    )


def crossed_left(table):
    high, low = halves(table)
    return np.concatenate(
        [np.concatenate([high, high], axis=1), np.concatenate([low, np.zeros_like(low)], axis=1)], axis=0
    )


def stacked(table):
    high, low = halves(table)
    return np.concatenate([high, high, low], axis=0)


def spaced(real, imag):
    out = np.zeros((real.shape[0], LANES))
    out[:, : real.shape[1]] = real
    out[:, HALF : HALF + imag.shape[1]] = imag
    return out


def make_tables(height, src_devices):
    rows = height // src_devices
    pixels = np.arange(height)
    angles = 2.0 * np.pi * (((np.arange(K) - K // 2)[:, None] * pixels[None, :]) % height) / height
    scaling = 1.0 / math.sqrt(height * KP)
    fc, fs = np.cos(angles) * scaling, -np.sin(angles) * scaling
    coarse = np.arange(N)
    back = 2.0 * np.pi * ((coarse[:, None] * (np.arange(KP) - KP // 2)[None, :]) % N) / N
    bc, bs = np.cos(back), np.sin(back)
    band = np.arange(1, KP)
    step = height // N
    delta = (pixels[:, None] - step * coarse[None, :]) % height
    up = (1.0 + 2.0 * np.cos(2.0 * np.pi * ((delta[..., None] * band) % height) / height).sum(-1)) / N

    both = np.concatenate([fc, fs], axis=0)
    row_in = np.stack([thrice(both[:, s * rows : (s + 1) * rows]) for s in range(src_devices)])
    col_in = beside(spaced(fc.T, fs.T))
    half_in = np.zeros((LANES, LANES))
    half_in[:KP] = np.concatenate([bc.T, bs.T], axis=1)
    half_in[HALF : HALF + KP] = np.concatenate([-bs.T, bc.T], axis=1)
    half_in = stacked(np.concatenate([half_in, -half_in[:, HALF:], half_in[:, :HALF]], axis=1))
    field_in = thrice(np.concatenate([bc, bs], axis=1))
    up_rows = thrice(up)
    high, low = halves(up.T)
    up_cols = np.concatenate([high, high, low, np.zeros_like(low)], axis=0)
    down_cols = crossed(up)
    down_rows = above(up.T)
    field_back = thrice(np.concatenate([bc.T, bs.T], axis=0))
    half_back = stacked(np.concatenate([spaced(bc, -bs), spaced(bs, bc)], axis=0))
    col_back = np.zeros((LANES, height))
    col_back[:K], col_back[HALF : HALF + K] = fc, fs
    col_back = stacked(col_back)
    row_back = np.stack([crossed_left(both[:, s * rows : (s + 1) * rows].T) for s in range(src_devices)])
    return dict(
        row_in=row_in, col_in=col_in, half_in=half_in, field_in=field_in, up_rows=up_rows, up_cols=up_cols,
        down_cols=down_cols, down_rows=down_rows, field_back=field_back, half_back=half_back,
        col_back=col_back, row_back=row_back,
    )


ORDER = (
    "row_in", "col_in", "half_in", "field_in", "up_rows", "up_cols",
    "down_cols", "down_rows", "field_back", "half_back", "col_back", "row_back",
)
PER_SOURCE = ("row_in", "row_back")


def mm(left, right):
    return jnp.dot(left, right, preferred_element_type=f32)


def split(value):
    high = value.astype(bf16)
    return high, (value - high.astype(f32)).astype(bf16)


def times_stacked(value, table):
    high, low = split(value)
    return mm(jnp.concatenate([high, low, high], axis=1), table)


def times_crossed(value, table):
    return mm(jnp.concatenate(split(value), axis=1), table)


def table_thrice(table, value):
    high, low = split(value)
    return mm(table, jnp.concatenate([high, high, low], axis=0))


def kernel(
    src_devices, clip_devices, scale,
    shifts_hbm, weights_hbm, masks_hbm, pupils_hbm, labels_hbm, *rest,
):
    count = len(ORDER)
    table_hbm = dict(zip(ORDER, rest[:count]))
    mask_out, term_out = rest[count : count + 2]
    tables = dict(zip(ORDER, rest[count + 2 : 2 * count + 2]))
    (
        shifts, weights, masks, pupils, labels, pupil_real, pupil_imag, fields, padded, total,
        spec_slots, shift_slots, weight_slots, shift_words, term_slots,
        local_sems, spec_send, spec_recv, small_send, small_recv,
        term_send, term_recv, result, term_result, out_sems,
    ) = rest[2 * count + 2 :]
    me = lax.axis_index("src")
    my_clip = lax.axis_index("clip")

    def bring(name):
        source = table_hbm[name]
        if name in PER_SOURCE:
            source = source.at[me]
        return pltpu.make_async_copy(source, tables[name], local_sems.at[ORDER.index(name)])

    copy_masks = pltpu.make_async_copy(masks_hbm, masks, local_sems.at[count])
    copy_pupils = pltpu.make_async_copy(pupils_hbm, pupils, local_sems.at[count + 1])
    copy_labels = pltpu.make_async_copy(labels_hbm, labels, local_sems.at[count + 2])
    copy_shifts = pltpu.make_async_copy(shifts_hbm, shifts, local_sems.at[count + 3])
    copy_weights = pltpu.make_async_copy(weights_hbm, weights, local_sems.at[count + 4])
    copies = {name: bring(name) for name in ORDER}
    copy_masks.start()
    copies["row_in"].start()
    copies["col_in"].start()

    barrier = pltpu.get_barrier_semaphore()
    for d in range(1, src_devices):
        pl.semaphore_signal(
            barrier, inc=1, device_id={"src": lax.rem(me + d, src_devices)}, device_id_type=pl.DeviceIdType.MESH
        )
    for d in range(1, clip_devices):
        pl.semaphore_signal(
            barrier, inc=1, device_id={"clip": lax.rem(my_clip + d, clip_devices)},
            device_id_type=pl.DeviceIdType.MESH,
        )

    copy_pupils.start()
    copy_shifts.start()
    copy_weights.start()
    for name in ORDER[2:6]:
        copies[name].start()
    copy_labels.start()
    for name in ORDER[6:]:
        copies[name].start()

    def exchange(axis, devices, mine, slots, send, recv):
        sent = []
        for d in range(1, devices):
            copy = pltpu.make_async_remote_copy(
                src_ref=slots.at[mine], dst_ref=slots.at[mine],
                send_sem=send.at[d - 1], recv_sem=recv.at[d - 1],
                device_id={axis: lax.rem(mine + d, devices)}, device_id_type=pl.DeviceIdType.MESH,
            )
            copy.start()
            sent.append(copy)
        return sent

    def arrive(sent):
        for copy in sent:
            copy.wait_recv()

    def add_slots(slots, devices):
        value = slots[0]
        for d in range(1, devices):
            value = value + slots[d]
        return value

    lane = lax.broadcasted_iota(jnp.int32, (1, LANES), 1)
    low_half = lane < HALF
    sign = jnp.where(low_half, -1.0, 1.0).astype(f32)

    def rotate(value):
        return pltpu.roll(value, HALF, 1) * sign

    copy_shifts.wait()
    copy_weights.wait()
    shift_slots[me] = jnp.broadcast_to(jnp.where(lane == 0, shifts[0, 0], shifts[0, 1]), (8, LANES))
    weight_slots[me] = jnp.full((8, LANES), weights[0], f32)

    copy_masks.wait()
    copies["row_in"].wait()
    copies["col_in"].wait()
    height = masks.shape[2]
    colors = range(2)
    sources = range(src_devices)
    spec_sent, small_sent = [], []
    for k in colors:
        rows_done = table_thrice(tables["row_in"][...], masks[k])
        pair = mm(jnp.concatenate(split(rows_done), axis=0), tables["col_in"][...])
        done = pair[: 2 * K, :LANES] + pair[: 2 * K, LANES:] + pair[2 * K :, :LANES]
        spec_slots[k, me] = done[:K] + rotate(done[K:])
        if k == 0:
            pl.semaphore_wait(barrier, src_devices + clip_devices - 2)
        spec_sent.append(
            exchange("src", src_devices, me, spec_slots.at[k], spec_send.at[k], spec_recv.at[k])
        )
        if k == 0:
            small_sent = exchange("src", src_devices, me, shift_slots, small_send.at[0], small_recv.at[0])
            small_sent += exchange("src", src_devices, me, weight_slots, small_send.at[1], small_recv.at[1])

    copy_pupils.wait()
    channels = pupils.shape[0]
    blank = jnp.zeros((KP, HALF - KP), f32)
    for c in range(channels):
        pr, pi = pupils[c, 0], pupils[c, 1]
        pupil_real[c] = jnp.concatenate([pr, blank, pr, blank], axis=1)
        pupil_imag[c] = jnp.concatenate([pi, blank, pi, blank], axis=1)
    padded[...] = jnp.zeros_like(padded)
    arrive(small_sent)
    copy_words = pltpu.make_async_copy(shift_slots, shift_words, local_sems.at[count + 5])
    copy_words.start()
    copies["half_in"].wait()
    copies["field_in"].wait()
    copy_words.wait()
    first = [shift_words[s, 0, 0] for s in sources]
    second = [shift_words[s, 0, 1] for s in sources]
    weight = [weight_slots[s, 0:1, :] for s in sources]

    coarse, own = [], []
    for k in colors:
        arrive(spec_sent[k])
        total[k] = add_slots(spec_slots.at[k], src_devices)
        summed_power = jnp.zeros((N, LANES), f32)
        own_power = jnp.zeros((N, LANES), f32)
        for s in sources:
            window = pltpu.roll(total[k, pl.ds(first[s], KP), :], lax.rem(LANES - second[s], LANES), 1)
            turned = rotate(window)
            products = [pupil_real[c] * window + pupil_imag[c] * turned for c in range(channels)]
            both = times_stacked(jnp.concatenate(products, axis=0), tables["half_in"][...])
            half_high, half_low = split(both[:, :LANES])
            turn_high, turn_low = split(both[:, LANES:])
            columns = []
            for c in range(channels):
                rows = slice(c * KP, (c + 1) * KP)
                columns.append(
                    jnp.concatenate(
                        [half_high[rows], turn_high[rows], half_high[rows], turn_high[rows], half_low[rows], turn_low[rows]],
                        axis=0,
                    )
                )
            wide = mm(tables["field_in"][...], jnp.concatenate(columns, axis=1))
            fields[k, s] = wide
            squares = wide * wide
            summed = squares[:, :LANES]
            for c in range(1, channels):
                summed = summed + squares[:, c * LANES : (c + 1) * LANES]
            power = (summed + pltpu.roll(summed, HALF, 1)) * (1.0 / (channels * src_devices))
            summed_power = summed_power + power * weight[s]
            own_power = own_power + jnp.where(me == s, power, 0.0)
        coarse.append(summed_power)
        own.append(own_power)
    copies["up_rows"].wait()
    copies["up_cols"].wait()
    copy_labels.wait()
    for name in ORDER[6:]:
        copies[name].wait()

    term = jnp.zeros((1, LANES), f32)
    slopes = []
    for k in colors:
        tall = table_thrice(tables["up_rows"][...], coarse[k])
        thin = []
        for r in range(0, height, CHUNK):
            part = tall[r : r + CHUNK]
            high = part.astype(bf16)
            wide_high = high.astype(f32)
            mixed = jnp.where(low_half, wide_high, part - wide_high).astype(bf16)
            intensity = mm(jnp.concatenate([mixed, high], axis=1), tables["up_cols"][...])
            level = jnp.tanh((0.5 * steepness) * (intensity - threshold))
            shifted = level + jnp.where(labels[r : r + CHUNK, :] == k + 1, -1.0, 1.0)
            slope = (0.25 * loss_weight * steepness) * shifted * (1.0 - level * level)
            thin.append(times_crossed(slope, tables["down_cols"][...]))
        thin = jnp.concatenate(split(jnp.concatenate(thin, axis=0)), axis=1)
        pair = mm(tables["down_rows"][...], thin)
        slope = pair[:N, :LANES] + pair[N:, :LANES] + pair[:N, LANES:]
        slope = slope + pltpu.roll(slope, HALF, 1)
        term = term + jnp.sum(slope * own[k], axis=0, keepdims=True)
        slopes.append(slope)
    term_slots[my_clip] = jnp.broadcast_to(0.5 * jnp.sum(term, axis=1, keepdims=True), (8, LANES))
    term_sent = exchange("clip", clip_devices, my_clip, term_slots, term_send, term_recv)

    leaving = []
    for k in colors:
        gathered = jnp.zeros((K, LANES), f32)
        for s in sources:
            slope = slopes[k] * (weight[s] * (2.0 / (channels * src_devices)))
            field_grad = fields[k, s] * jnp.concatenate([slope] * channels, axis=1)
            back = table_thrice(tables["field_back"][...], field_grad)
            pieces = []
            for c in range(channels):
                block = back[:, c * LANES : (c + 1) * LANES]
                pieces.append(block[:KP] - rotate(block[KP:]))
            product_grad = times_stacked(jnp.concatenate(pieces, axis=0), tables["half_back"][...])
            along = jnp.zeros((KP, LANES), f32)
            across = jnp.zeros((KP, LANES), f32)
            for c in range(channels):
                block = product_grad[c * KP : (c + 1) * KP]
                along = along + pupil_real[c] * block
                across = across + pupil_imag[c] * block
            window_grad = along - rotate(across)
            padded[k, s, K - KP : K, :] = pltpu.roll(window_grad, second[s], 1)
            gathered = gathered + padded[k, s, pl.ds(K - KP - first[s], K), :]

        turned = jnp.concatenate([gathered, -rotate(gathered)], axis=0)
        folded = times_stacked(turned, tables["col_back"][...])
        pair = mm(tables["row_back"][...], jnp.concatenate(split(folded), axis=0))
        plane = masks[k]
        pull = (4.0 * binarize) * (1.0 - plane * plane) * plane
        result[k] = pair[: result.shape[1]] + pair[result.shape[1] :] - pull
        leaving.append(pltpu.make_async_copy(result.at[k], mask_out.at[k], out_sems.at[k]))
        leaving[-1].start()
        if k == 0:
            arrive(term_sent)
            summed = add_slots(term_slots, clip_devices)
            term_result[0] = jnp.sum(jnp.where(lane == 0, summed[:1], 0.0)) * scale
            leaving.append(pltpu.make_async_copy(term_result, term_out, out_sems.at[2]))
            leaving[-1].start()
            for sent in spec_sent + [small_sent, term_sent]:
                for copy in sent:
                    copy.wait_send()
    for copy in leaving:
        copy.wait()


def hand_on(mask_in, term_in, mask_out, term_out, held, term_held, sems):
    colors = range(mask_in.shape[0])
    arriving = [pltpu.make_async_copy(mask_in.at[k], held.at[k], sems.at[k]) for k in colors]
    leaving = [pltpu.make_async_copy(held.at[k], mask_out.at[k], sems.at[2 + k]) for k in colors]
    arriving.append(pltpu.make_async_copy(term_in, term_held, sems.at[4]))
    leaving.append(pltpu.make_async_copy(term_held, term_out, sems.at[5]))
    for copy in arriving:
        copy.start()
    for before, after in zip(arriving, leaving):
        before.wait()
        after.start()
    for copy in leaving:
        copy.wait()


def per_device(color_masks, source_weights, pupil_shifts, pupils, target_labels):
    src_devices = lax.axis_size("src")
    clip_devices = lax.axis_size("clip")
    rows, height = color_masks.shape[2], color_masks.shape[3]
    channels = pupils.shape[0]
    tables = make_tables(height, src_devices)
    masks_here = color_masks[0]
    scale = src_devices / (2.0 * clip_devices * height * height)
    operands = [jnp.asarray(tables[name]) for name in ORDER]
    table_scratch = []
    for name in ORDER:
        shape = tables[name].shape[1:] if name in PER_SOURCE else tables[name].shape
        table_scratch.append(pltpu.VMEM(shape, bf16))
    far = pl.BlockSpec(memory_space=pltpu.HBM)
    dma = pltpu.SemaphoreType.DMA
    mask_grad, terms = pl.pallas_call(
        functools.partial(kernel, src_devices, clip_devices, scale),
        out_shape=(
            jax.ShapeDtypeStruct((2, rows, height), f32),
            jax.ShapeDtypeStruct((1,), f32),
        ),
        in_specs=[far] * (5 + len(ORDER)),
        out_specs=(far, far),
        scratch_shapes=table_scratch
        + [
            pltpu.SMEM((1, 2), jnp.int32),
            pltpu.SMEM((1,), f32),
            pltpu.VMEM((2, rows, height), f32),
            pltpu.VMEM(pupils.shape, f32),
            pltpu.VMEM((height, height), jnp.int32),
            pltpu.VMEM((channels, KP, LANES), f32),
            pltpu.VMEM((channels, KP, LANES), f32),
            pltpu.VMEM((2, src_devices, N, channels * LANES), f32),
            pltpu.VMEM((2, src_devices, 2 * K - KP, LANES), f32),
            pltpu.VMEM((2, K, LANES), f32),
            pltpu.VMEM((2, src_devices, K, LANES), f32),
            pltpu.VMEM((src_devices, 8, LANES), jnp.int32),
            pltpu.VMEM((src_devices, 8, LANES), f32),
            pltpu.SMEM((src_devices, 8, LANES), jnp.int32),
            pltpu.VMEM((clip_devices, 8, LANES), f32),
            dma((len(ORDER) + 6,)),
        ]
        + [dma((2, src_devices - 1))] * 4
        + [dma((clip_devices - 1,))] * 2
        + [pltpu.VMEM((2, rows, height), f32), pltpu.SMEM((1,), f32), dma((3,))],
        compiler_params=pltpu.CompilerParams(
            collective_id=0, has_side_effects=True, vmem_limit_bytes=60 * 1024 * 1024
        ),
        name="abbe_gradient",
    )(pupil_shifts, source_weights, masks_here, pupils, target_labels[0], *operands)
    mask_grad, terms = pl.pallas_call(
        hand_on,
        out_shape=(
            jax.ShapeDtypeStruct((2, rows, height), f32),
            jax.ShapeDtypeStruct((1,), f32),
        ),
        in_specs=[far, far],
        out_specs=(far, far),
        scratch_shapes=[pltpu.VMEM((2, rows, height), f32), pltpu.SMEM((1,), f32), dma((6,))],
        compiler_params=pltpu.CompilerParams(vmem_limit_bytes=60 * 1024 * 1024),
        name="hand_on",
    )(mask_grad, terms)
    return mask_grad[None], terms


def solution(mesh):
    in_specs = (P("clip", None, "src", None), P("src"), P("src", None), P(), P("clip", None, None))
    out_specs = (P("clip", None, "src", None), P("src"))
    return jax.shard_map(
        per_device, mesh=mesh, in_specs=in_specs, out_specs=out_specs, check_vma=False
    )
```

```python
import functools
import math

import jax
import jax.numpy as jnp
import ml_dtypes
import numpy as np
from jax import lax
from jax.experimental import pallas as pl
from jax.experimental.pallas import tpu as pltpu
from jax.sharding import PartitionSpec as P

K = 48
KP = 32
N = 2 * KP
LANES = 128
HALF = 64
CHUNK = 64

steepness = 4.0
threshold = 0.6
loss_weight = 2.0
binarize = 0.25
f32 = jnp.float32
bf16 = jnp.bfloat16


def halves(table):
    high = table.astype(np.float32).astype(ml_dtypes.bfloat16)
    low = (table - high.astype(np.float64)).astype(np.float32).astype(ml_dtypes.bfloat16)
    return high, low


def beside(table):
    return np.concatenate(halves(table), axis=-1)


def above(table):
    return np.concatenate(halves(table), axis=-2)


def thrice(table):
    high, low = halves(table)
    return np.concatenate([high, low, high], axis=-1)


def crossed(table):
    high, low = halves(table)
    return np.concatenate(
        [np.concatenate([high, low], axis=1), np.concatenate([high, np.zeros_like(low)], axis=1)], axis=0
    )


def crossed_left(table):
    high, low = halves(table)
    return np.concatenate(
        [np.concatenate([high, high], axis=1), np.concatenate([low, np.zeros_like(low)], axis=1)], axis=0
    )


def spaced(real, imag):
    out = np.zeros((real.shape[0], LANES))
    out[:, : real.shape[1]] = real
    out[:, HALF : HALF + imag.shape[1]] = imag
    return out


def make_tables(height, src_devices):
    rows = height // src_devices
    pixels = np.arange(height)
    angles = 2.0 * np.pi * (((np.arange(K) - K // 2)[:, None] * pixels[None, :]) % height) / height
    scaling = 1.0 / math.sqrt(height * KP)
    fc, fs = np.cos(angles) * scaling, -np.sin(angles) * scaling
    coarse = np.arange(N)
    back = 2.0 * np.pi * ((coarse[:, None] * (np.arange(KP) - KP // 2)[None, :]) % N) / N
    bc, bs = np.cos(back), np.sin(back)
    band = np.arange(1, KP)
    step = height // N
    delta = (pixels[:, None] - step * coarse[None, :]) % height
    up = (1.0 + 2.0 * np.cos(2.0 * np.pi * ((delta[..., None] * band) % height) / height).sum(-1)) / N

    both = np.concatenate([fc, fs], axis=0)
    row_in = np.stack([thrice(both[:, s * rows : (s + 1) * rows]) for s in range(src_devices)])
    col_in = beside(spaced(fc.T, fs.T))
    half_in = np.zeros((LANES, LANES))
    half_in[:KP] = np.concatenate([bc.T, bs.T], axis=1)
    half_in[HALF : HALF + KP] = np.concatenate([-bs.T, bc.T], axis=1)
    half_in = crossed(half_in)
    field_in = thrice(np.concatenate([bc, bs], axis=1))
    up_rows = thrice(up)
    high, low = halves(up.T)
    up_cols = np.concatenate([high, high, low, np.zeros_like(low)], axis=0)
    down_cols = crossed(up)
    down_rows = above(up.T)
    field_back = thrice(np.concatenate([bc.T, bs.T], axis=0))
    half_back = crossed(np.concatenate([spaced(bc, -bs), spaced(bs, bc)], axis=0))
    col_back = np.zeros((LANES, height))
    col_back[:K], col_back[HALF : HALF + K] = fc, fs
    high, low = halves(col_back)
    col_back = np.concatenate([high, high, low], axis=0)
    row_back = np.stack([crossed_left(both[:, s * rows : (s + 1) * rows].T) for s in range(src_devices)])
    return dict(
        row_in=row_in, col_in=col_in, half_in=half_in, field_in=field_in, up_rows=up_rows, up_cols=up_cols,
        down_cols=down_cols, down_rows=down_rows, field_back=field_back, half_back=half_back,
        col_back=col_back, row_back=row_back,
    )


ORDER = (
    "row_in", "col_in", "half_in", "field_in", "up_rows", "up_cols",
    "down_cols", "down_rows", "field_back", "half_back", "col_back", "row_back",
)
PER_SOURCE = ("row_in", "row_back")


def mm(left, right):
    return jnp.dot(left, right, preferred_element_type=f32)


def split(value):
    high = value.astype(bf16)
    return high, (value - high.astype(f32)).astype(bf16)


def add_halves(value):
    width = value.shape[1] // 2
    return value[:, :width] + value[:, width:]


def times_crossed(value, table):
    return mm(jnp.concatenate(split(value), axis=1), table)


def table_thrice(table, value):
    high, low = split(value)
    return mm(table, jnp.concatenate([high, high, low], axis=0))


def kernel(
    src_devices, clip_devices, scale,
    shifts_hbm, weights_hbm, masks_hbm, pupils_hbm, labels_hbm, *rest,
):
    count = len(ORDER)
    table_hbm = dict(zip(ORDER, rest[:count]))
    mask_out, term_out = rest[count : count + 2]
    tables = dict(zip(ORDER, rest[count + 2 : 2 * count + 2]))
    (
        shifts, weights, masks, pupils, labels, pupil_real, pupil_imag, fields, padded, total,
        spec_slots, power_slots, grad_slots, term_slots,
        local_sems, spec_send, spec_recv, power_send, power_recv,
        grad_send, grad_recv, term_send, term_recv, result, term_result, out_sems,
    ) = rest[2 * count + 2 :]
    me = lax.axis_index("src")
    my_clip = lax.axis_index("clip")

    barrier = pltpu.get_barrier_semaphore()
    for d in range(1, src_devices):
        pl.semaphore_signal(
            barrier, inc=1, device_id={"src": lax.rem(me + d, src_devices)}, device_id_type=pl.DeviceIdType.MESH
        )
    for d in range(1, clip_devices):
        pl.semaphore_signal(
            barrier, inc=1, device_id={"clip": lax.rem(my_clip + d, clip_devices)},
            device_id_type=pl.DeviceIdType.MESH,
        )

    def bring(name):
        source = table_hbm[name]
        if name in PER_SOURCE:
            source = source.at[me]
        return pltpu.make_async_copy(source, tables[name], local_sems.at[ORDER.index(name)])

    copy_masks = pltpu.make_async_copy(masks_hbm, masks, local_sems.at[count])
    copy_pupils = pltpu.make_async_copy(pupils_hbm, pupils, local_sems.at[count + 1])
    copy_labels = pltpu.make_async_copy(labels_hbm, labels, local_sems.at[count + 2])
    copy_shifts = pltpu.make_async_copy(shifts_hbm, shifts, local_sems.at[count + 3])
    copy_weights = pltpu.make_async_copy(weights_hbm, weights, local_sems.at[count + 4])
    copies = {name: bring(name) for name in ORDER}
    copy_masks.start()
    copies["row_in"].start()
    copies["col_in"].start()

    copy_pupils.start()
    copy_shifts.start()
    copy_weights.start()
    for name in ORDER[2:6]:
        copies[name].start()
    copy_labels.start()
    for name in ORDER[6:]:
        copies[name].start()

    def exchange(axis, devices, mine, slots, send, recv):
        sent = []
        for d in range(1, devices):
            copy = pltpu.make_async_remote_copy(
                src_ref=slots.at[mine], dst_ref=slots.at[mine],
                send_sem=send.at[d - 1], recv_sem=recv.at[d - 1],
                device_id={axis: lax.rem(mine + d, devices)}, device_id_type=pl.DeviceIdType.MESH,
            )
            copy.start()
            sent.append(copy)
        return sent

    def arrive(sent):
        for copy in sent:
            copy.wait_recv()

    def add_slots(slots, devices):
        value = slots[0]
        for d in range(1, devices):
            value = value + slots[d]
        return value

    lane = lax.broadcasted_iota(jnp.int32, (1, LANES), 1)
    low_half = lane < HALF
    sign = jnp.where(low_half, -1.0, 1.0).astype(f32)

    def rotate(value):
        return pltpu.roll(value, HALF, 1) * sign

    copy_masks.wait()
    copies["row_in"].wait()
    copies["col_in"].wait()
    height = masks.shape[2]
    colors = range(2)
    spec_sent, power_sent, grad_sent = [], [], []
    for k in colors:
        rows_done = table_thrice(tables["row_in"][...], masks[k])
        pair = mm(jnp.concatenate(split(rows_done), axis=0), tables["col_in"][...])
        done = pair[: 2 * K, :LANES] + pair[: 2 * K, LANES:] + pair[2 * K :, :LANES]
        spec_slots[k, me] = done[:K] + rotate(done[K:])
        if k == 0:
            pl.semaphore_wait(barrier, src_devices + clip_devices - 2)
        spec_sent.append(
            exchange("src", src_devices, me, spec_slots.at[k], spec_send.at[k], spec_recv.at[k])
        )

    copy_pupils.wait()
    channels = pupils.shape[0]
    blank = jnp.zeros((KP, HALF - KP), f32)
    for c in range(channels):
        pr, pi = pupils[c, 0], pupils[c, 1]
        pupil_real[c] = jnp.concatenate([pr, blank, pr, blank], axis=1)
        pupil_imag[c] = jnp.concatenate([pi, blank, pi, blank], axis=1)
    padded[...] = jnp.zeros_like(padded)
    copy_shifts.wait()
    copy_weights.wait()
    first = shifts[0, 0]
    second = shifts[0, 1]
    weight = weights[0]
    copies["half_in"].wait()
    copies["field_in"].wait()

    raw = []
    for k in colors:
        arrive(spec_sent[k])
        total[k] = add_slots(spec_slots.at[k], src_devices)
        window = pltpu.roll(total[k, pl.ds(first, KP), :], lax.rem(LANES - second, LANES), 1)
        turned = rotate(window)
        products = [pupil_real[c] * window + pupil_imag[c] * turned for c in range(channels)]
        half = add_halves(times_crossed(jnp.concatenate(products, axis=0), tables["half_in"][...]))
        half_high, half_low = split(half)
        turn_high, turn_low = split(rotate(half))
        columns = []
        for c in range(channels):
            rows = slice(c * KP, (c + 1) * KP)
            columns.append(
                jnp.concatenate(
                    [half_high[rows], turn_high[rows], half_high[rows], turn_high[rows], half_low[rows], turn_low[rows]],
                    axis=0,
                )
            )
        wide = mm(tables["field_in"][...], jnp.concatenate(columns, axis=1))
        fields[k] = wide
        squares = wide * wide
        summed = squares[:, :LANES]
        for c in range(1, channels):
            summed = summed + squares[:, c * LANES : (c + 1) * LANES]
        power = (summed + pltpu.roll(summed, HALF, 1)) * (1.0 / (channels * src_devices))
        raw.append(power)
        power_slots[k, me] = jnp.where(low_half, power[: N // 2], power[N // 2 :]) * weight
        power_sent.append(
            exchange("src", src_devices, me, power_slots.at[k], power_send.at[k], power_recv.at[k])
        )
    copies["up_rows"].wait()
    copies["up_cols"].wait()
    copy_labels.wait()
    for name in ORDER[6:]:
        copies[name].wait()

    term = jnp.zeros((1, LANES), f32)
    for k in colors:
        arrive(power_sent[k])
        packed = add_slots(power_slots.at[k], src_devices)
        turned = pltpu.roll(packed, HALF, 1)
        coarse = jnp.concatenate(
            [jnp.where(low_half, packed, turned), jnp.where(low_half, turned, packed)], axis=0
        )
        tall = table_thrice(tables["up_rows"][...], coarse)
        thin = []
        for r in range(0, height, CHUNK):
            part = tall[r : r + CHUNK]
            high = part.astype(bf16)
            wide_high = high.astype(f32)
            mixed = jnp.where(low_half, wide_high, part - wide_high).astype(bf16)
            intensity = mm(jnp.concatenate([mixed, high], axis=1), tables["up_cols"][...])
            level = jnp.tanh((0.5 * steepness) * (intensity - threshold))
            shifted = level + jnp.where(labels[r : r + CHUNK, :] == k + 1, -1.0, 1.0)
            slope = (0.25 * loss_weight * steepness) * shifted * (1.0 - level * level)
            thin.append(times_crossed(slope, tables["down_cols"][...]))
        thin = jnp.concatenate(split(jnp.concatenate(thin, axis=0)), axis=1)
        pair = mm(tables["down_rows"][...], thin)
        slope = pair[:N, :LANES] + pair[N:, :LANES] + pair[:N, LANES:]
        slope = slope + pltpu.roll(slope, HALF, 1)
        term = term + jnp.sum(slope * raw[k], axis=0, keepdims=True)
        if k == 1:
            term_slots[my_clip] = jnp.broadcast_to(0.5 * jnp.sum(term, axis=1, keepdims=True), (8, LANES))
            term_sent = exchange("clip", clip_devices, my_clip, term_slots, term_send, term_recv)

        slope = slope * (weight * (2.0 / (channels * src_devices)))
        field_grad = fields[k] * jnp.concatenate([slope] * channels, axis=1)
        back = table_thrice(tables["field_back"][...], field_grad)
        pieces = []
        for c in range(channels):
            block = back[:, c * LANES : (c + 1) * LANES]
            pieces.append(block[:KP] - rotate(block[KP:]))
        product_grad = add_halves(times_crossed(jnp.concatenate(pieces, axis=0), tables["half_back"][...]))
        along = jnp.zeros((KP, LANES), f32)
        across = jnp.zeros((KP, LANES), f32)
        for c in range(channels):
            block = product_grad[c * KP : (c + 1) * KP]
            along = along + pupil_real[c] * block
            across = across + pupil_imag[c] * block
        window_grad = along - rotate(across)
        padded[k, K - KP : K, :] = pltpu.roll(window_grad, second, 1)
        grad_slots[k, me] = padded[k, pl.ds(K - KP - first, K), :]
        grad_sent.append(
            exchange("src", src_devices, me, grad_slots.at[k], grad_send.at[k], grad_recv.at[k])
        )

    leaving = []
    for k in colors:
        if k == 1:
            for sent in spec_sent + power_sent + grad_sent[:1] + [term_sent]:
                for copy in sent:
                    copy.wait_send()
        arrive(grad_sent[k])
        gathered = add_slots(grad_slots.at[k], src_devices)
        high, low = split(jnp.concatenate([gathered, -rotate(gathered)], axis=0))
        folded = mm(jnp.concatenate([high, low, high], axis=1), tables["col_back"][...])
        pair = mm(tables["row_back"][...], jnp.concatenate(split(folded), axis=0))
        plane = masks[k]
        pull = (4.0 * binarize) * (1.0 - plane * plane) * plane
        result[k] = pair[: result.shape[1]] + pair[result.shape[1] :] - pull
        leaving.append(pltpu.make_async_copy(result.at[k], mask_out.at[k], out_sems.at[k]))
        leaving[-1].start()
        if k == 0:
            arrive(term_sent)
            summed = add_slots(term_slots, clip_devices)
            term_result[0] = jnp.sum(jnp.where(lane == 0, summed[:1], 0.0)) * scale
            leaving.append(pltpu.make_async_copy(term_result, term_out, out_sems.at[2]))
            leaving[-1].start()
    for copy in grad_sent[1]:
        copy.wait_send()
    for copy in leaving:
        copy.wait()


def hand_on(mask_in, term_in, mask_out, term_out, held, term_held, sems):
    colors = range(mask_in.shape[0])
    arriving = [pltpu.make_async_copy(mask_in.at[k], held.at[k], sems.at[k]) for k in colors]
    leaving = [pltpu.make_async_copy(held.at[k], mask_out.at[k], sems.at[2 + k]) for k in colors]
    arriving.append(pltpu.make_async_copy(term_in, term_held, sems.at[4]))
    leaving.append(pltpu.make_async_copy(term_held, term_out, sems.at[5]))
    for copy in arriving:
        copy.start()
    for before, after in zip(arriving, leaving):
        before.wait()
        after.start()
    for copy in leaving:
        copy.wait()


def per_device(color_masks, source_weights, pupil_shifts, pupils, target_labels):
    src_devices = lax.axis_size("src")
    clip_devices = lax.axis_size("clip")
    rows, height = color_masks.shape[2], color_masks.shape[3]
    channels = pupils.shape[0]
    tables = make_tables(height, src_devices)
    masks_here = color_masks[0]
    scale = src_devices / (2.0 * clip_devices * height * height)
    operands = [jnp.asarray(tables[name]) for name in ORDER]
    table_scratch = []
    for name in ORDER:
        shape = tables[name].shape[1:] if name in PER_SOURCE else tables[name].shape
        table_scratch.append(pltpu.VMEM(shape, bf16))
    far = pl.BlockSpec(memory_space=pltpu.HBM)
    dma = pltpu.SemaphoreType.DMA
    mask_grad, terms = pl.pallas_call(
        functools.partial(kernel, src_devices, clip_devices, scale),
        out_shape=(
            jax.ShapeDtypeStruct((2, rows, height), f32),
            jax.ShapeDtypeStruct((1,), f32),
        ),
        in_specs=[far] * (5 + len(ORDER)),
        out_specs=(far, far),
        scratch_shapes=table_scratch
        + [
            pltpu.SMEM((1, 2), jnp.int32),
            pltpu.SMEM((1,), f32),
            pltpu.VMEM((2, rows, height), f32),
            pltpu.VMEM(pupils.shape, f32),
            pltpu.VMEM((height, height), jnp.int32),
            pltpu.VMEM((channels, KP, LANES), f32),
            pltpu.VMEM((channels, KP, LANES), f32),
            pltpu.VMEM((2, N, channels * LANES), f32),
            pltpu.VMEM((2, 2 * K - KP, LANES), f32),
            pltpu.VMEM((2, K, LANES), f32),
            pltpu.VMEM((2, src_devices, K, LANES), f32),
            pltpu.VMEM((2, src_devices, N // 2, LANES), f32),
            pltpu.VMEM((2, src_devices, K, LANES), f32),
            pltpu.VMEM((clip_devices, 8, LANES), f32),
            dma((len(ORDER) + 5,)),
        ]
        + [dma((2, src_devices - 1))] * 6
        + [dma((clip_devices - 1,))] * 2
        + [pltpu.VMEM((2, rows, height), f32), pltpu.SMEM((1,), f32), dma((3,))],
        compiler_params=pltpu.CompilerParams(
            collective_id=0, has_side_effects=True, vmem_limit_bytes=60 * 1024 * 1024
        ),
        name="abbe_gradient",
    )(pupil_shifts, source_weights, masks_here, pupils, target_labels[0], *operands)
    mask_grad, terms = pl.pallas_call(
        hand_on,
        out_shape=(
            jax.ShapeDtypeStruct((2, rows, height), f32),
            jax.ShapeDtypeStruct((1,), f32),
        ),
        in_specs=[far, far],
        out_specs=(far, far),
        scratch_shapes=[pltpu.VMEM((2, rows, height), f32), pltpu.SMEM((1,), f32), dma((6,))],
        compiler_params=pltpu.CompilerParams(vmem_limit_bytes=60 * 1024 * 1024),
        name="hand_on",
    )(mask_grad, terms)
    return mask_grad[None], terms


def solution(mesh):
    in_specs = (P("clip", None, "src", None), P("src"), P("src", None), P(), P("clip", None, None))
    out_specs = (P("clip", None, "src", None), P("src"))
    return jax.shard_map(
        per_device, mesh=mesh, in_specs=in_specs, out_specs=out_specs, check_vma=False
    )
```

```python
import functools
import math

import jax
import jax.numpy as jnp
import ml_dtypes
import numpy as np
from jax import lax
from jax.experimental import pallas as pl
from jax.experimental.pallas import tpu as pltpu
from jax.sharding import PartitionSpec as P

K = 48
KP = 32
N = 2 * KP
LANES = 128
HALF = 64
CHUNK = 256

steepness = 4.0
threshold = 0.6
loss_weight = 2.0
binarize = 0.25
f32 = jnp.float32
bf16 = jnp.bfloat16


def halves(table):
    high = table.astype(np.float32).astype(ml_dtypes.bfloat16)
    low = (table - high.astype(np.float64)).astype(np.float32).astype(ml_dtypes.bfloat16)
    return high, low


def beside(table):
    return np.concatenate(halves(table), axis=-1)


def above(table):
    return np.concatenate(halves(table), axis=-2)


def thrice(table):
    high, low = halves(table)
    return np.concatenate([high, low, high], axis=-1)


def crossed(table):
    high, low = halves(table)
    return np.concatenate(
        [np.concatenate([high, low], axis=1), np.concatenate([high, np.zeros_like(low)], axis=1)], axis=0
    )


def crossed_left(table):
    high, low = halves(table)
    return np.concatenate(
        [np.concatenate([high, high], axis=1), np.concatenate([low, np.zeros_like(low)], axis=1)], axis=0
    )


def spaced(real, imag):
    out = np.zeros((real.shape[0], LANES))
    out[:, : real.shape[1]] = real
    out[:, HALF : HALF + imag.shape[1]] = imag
    return out


def make_tables(height, src_devices):
    rows = height // src_devices
    pixels = np.arange(height)
    angles = 2.0 * np.pi * (((np.arange(K) - K // 2)[:, None] * pixels[None, :]) % height) / height
    scaling = 1.0 / math.sqrt(height * KP)
    fc, fs = np.cos(angles) * scaling, -np.sin(angles) * scaling
    coarse = np.arange(N)
    back = 2.0 * np.pi * ((coarse[:, None] * (np.arange(KP) - KP // 2)[None, :]) % N) / N
    bc, bs = np.cos(back), np.sin(back)
    band = np.arange(1, KP)
    step = height // N
    delta = (pixels[:, None] - step * coarse[None, :]) % height
    up = (1.0 + 2.0 * np.cos(2.0 * np.pi * ((delta[..., None] * band) % height) / height).sum(-1)) / N

    both = np.concatenate([fc, fs], axis=0)
    row_in = np.stack([thrice(both[:, s * rows : (s + 1) * rows]) for s in range(src_devices)])
    col_in = beside(spaced(fc.T, fs.T))
    half_in = np.zeros((LANES, LANES))
    half_in[:KP] = np.concatenate([bc.T, bs.T], axis=1)
    half_in[HALF : HALF + KP] = np.concatenate([-bs.T, bc.T], axis=1)
    half_in = crossed(half_in)
    field_in = thrice(np.concatenate([bc, bs], axis=1))
    up_rows = thrice(up)
    high, low = halves(up.T)
    up_cols = np.concatenate([high, high, low, np.zeros_like(low)], axis=0)
    down_cols = crossed(up)
    down_rows = above(up.T)
    field_back = thrice(np.concatenate([bc.T, bs.T], axis=0))
    half_back = crossed(np.concatenate([spaced(bc, -bs), spaced(bs, bc)], axis=0))
    col_back = np.zeros((LANES, height))
    col_back[:K], col_back[HALF : HALF + K] = fc, fs
    high, low = halves(col_back)
    col_back = np.concatenate([high, high, low], axis=0)
    row_back = np.stack([crossed_left(both[:, s * rows : (s + 1) * rows].T) for s in range(src_devices)])
    return dict(
        row_in=row_in, col_in=col_in, half_in=half_in, field_in=field_in, up_rows=up_rows, up_cols=up_cols,
        down_cols=down_cols, down_rows=down_rows, field_back=field_back, half_back=half_back,
        col_back=col_back, row_back=row_back,
    )


ORDER = (
    "row_in", "col_in", "half_in", "field_in", "up_rows", "up_cols",
    "down_cols", "down_rows", "field_back", "half_back", "col_back", "row_back",
)
PER_SOURCE = ("row_in", "row_back")


def mm(left, right):
    return jnp.dot(left, right, preferred_element_type=f32)


def split(value):
    high = value.astype(bf16)
    return high, (value - high.astype(f32)).astype(bf16)


def add_halves(value):
    width = value.shape[1] // 2
    return value[:, :width] + value[:, width:]


def times_crossed(value, table):
    return mm(jnp.concatenate(split(value), axis=1), table)


def table_thrice(table, value):
    high, low = split(value)
    return mm(table, jnp.concatenate([high, high, low], axis=0))


def kernel(
    src_devices, clip_devices, scale,
    shifts_hbm, weights_hbm, masks_hbm, pupils_hbm, labels_hbm, *rest,
):
    count = len(ORDER)
    table_hbm = dict(zip(ORDER, rest[:count]))
    mask_out, term_out = rest[count : count + 2]
    tables = dict(zip(ORDER, rest[count + 2 : 2 * count + 2]))
    (
        shifts, weights, masks, pupils, labels, pupil_real, pupil_imag, fields, padded, total,
        spec_slots, power_slots, grad_slots, term_slots,
        local_sems, spec_send, spec_recv, power_send, power_recv,
        grad_send, grad_recv, term_send, term_recv, result, term_result, out_sems,
    ) = rest[2 * count + 2 :]
    me = lax.axis_index("src")
    my_clip = lax.axis_index("clip")

    barrier = pltpu.get_barrier_semaphore()
    for d in range(1, src_devices):
        pl.semaphore_signal(
            barrier, inc=1, device_id={"src": lax.rem(me + d, src_devices)}, device_id_type=pl.DeviceIdType.MESH
        )
    for d in range(1, clip_devices):
        pl.semaphore_signal(
            barrier, inc=1, device_id={"clip": lax.rem(my_clip + d, clip_devices)},
            device_id_type=pl.DeviceIdType.MESH,
        )

    def bring(name):
        source = table_hbm[name]
        if name in PER_SOURCE:
            source = source.at[me]
        return pltpu.make_async_copy(source, tables[name], local_sems.at[ORDER.index(name)])

    copy_masks = pltpu.make_async_copy(masks_hbm, masks, local_sems.at[count])
    copy_pupils = pltpu.make_async_copy(pupils_hbm, pupils, local_sems.at[count + 1])
    copy_labels = pltpu.make_async_copy(labels_hbm, labels, local_sems.at[count + 2])
    copy_shifts = pltpu.make_async_copy(shifts_hbm, shifts, local_sems.at[count + 3])
    copy_weights = pltpu.make_async_copy(weights_hbm, weights, local_sems.at[count + 4])
    copies = {name: bring(name) for name in ORDER}
    copy_masks.start()
    copies["row_in"].start()
    copies["col_in"].start()

    copy_pupils.start()
    copy_shifts.start()
    copy_weights.start()
    for name in ORDER[2:6]:
        copies[name].start()
    copy_labels.start()
    for name in ORDER[6:]:
        copies[name].start()

    def exchange(axis, devices, mine, slots, send, recv):
        sent = []
        for d in range(1, devices):
            copy = pltpu.make_async_remote_copy(
                src_ref=slots.at[mine], dst_ref=slots.at[mine],
                send_sem=send.at[d - 1], recv_sem=recv.at[d - 1],
                device_id={axis: lax.rem(mine + d, devices)}, device_id_type=pl.DeviceIdType.MESH,
            )
            copy.start()
            sent.append(copy)
        return sent

    def arrive(sent):
        for copy in sent:
            copy.wait_recv()

    def add_slots(slots, devices):
        value = slots[0]
        for d in range(1, devices):
            value = value + slots[d]
        return value

    lane = lax.broadcasted_iota(jnp.int32, (1, LANES), 1)
    low_half = lane < HALF
    sign = jnp.where(low_half, -1.0, 1.0).astype(f32)

    def rotate(value):
        return pltpu.roll(value, HALF, 1) * sign

    copy_masks.wait()
    copies["row_in"].wait()
    copies["col_in"].wait()
    height = masks.shape[2]
    colors = range(2)
    spec_sent, power_sent, grad_sent = [], [], []
    for k in colors:
        rows_done = table_thrice(tables["row_in"][...], masks[k])
        pair = mm(jnp.concatenate(split(rows_done), axis=0), tables["col_in"][...])
        done = pair[: 2 * K, :LANES] + pair[: 2 * K, LANES:] + pair[2 * K :, :LANES]
        spec_slots[k, me] = done[:K] + rotate(done[K:])
        if k == 0:
            pl.semaphore_wait(barrier, src_devices + clip_devices - 2)
        spec_sent.append(
            exchange("src", src_devices, me, spec_slots.at[k], spec_send.at[k], spec_recv.at[k])
        )

    copy_pupils.wait()
    channels = pupils.shape[0]
    blank = jnp.zeros((KP, HALF - KP), f32)
    for c in range(channels):
        pr, pi = pupils[c, 0], pupils[c, 1]
        pupil_real[c] = jnp.concatenate([pr, blank, pr, blank], axis=1)
        pupil_imag[c] = jnp.concatenate([pi, blank, pi, blank], axis=1)
    padded[...] = jnp.zeros_like(padded)
    copy_shifts.wait()
    copy_weights.wait()
    first = shifts[0, 0]
    second = shifts[0, 1]
    weight = weights[0]
    copies["half_in"].wait()
    copies["field_in"].wait()

    raw = []
    for k in colors:
        arrive(spec_sent[k])
        total[k] = add_slots(spec_slots.at[k], src_devices)
        window = pltpu.roll(total[k, pl.ds(first, KP), :], lax.rem(LANES - second, LANES), 1)
        turned = rotate(window)
        products = [pupil_real[c] * window + pupil_imag[c] * turned for c in range(channels)]
        half = add_halves(times_crossed(jnp.concatenate(products, axis=0), tables["half_in"][...]))
        half_high, half_low = split(half)
        turn_high, turn_low = split(rotate(half))
        columns = []
        for c in range(channels):
            rows = slice(c * KP, (c + 1) * KP)
            columns.append(
                jnp.concatenate(
                    [half_high[rows], turn_high[rows], half_high[rows], turn_high[rows], half_low[rows], turn_low[rows]],
                    axis=0,
                )
            )
        wide = mm(tables["field_in"][...], jnp.concatenate(columns, axis=1))
        fields[k] = wide
        squares = wide * wide
        summed = squares[:, :LANES]
        for c in range(1, channels):
            summed = summed + squares[:, c * LANES : (c + 1) * LANES]
        power = (summed + pltpu.roll(summed, HALF, 1)) * (1.0 / (channels * src_devices))
        raw.append(power)
        power_slots[k, me] = jnp.where(low_half, power[: N // 2], power[N // 2 :]) * weight
        power_sent.append(
            exchange("src", src_devices, me, power_slots.at[k], power_send.at[k], power_recv.at[k])
        )
    copies["up_rows"].wait()
    copies["up_cols"].wait()
    copy_labels.wait()
    for name in ORDER[6:]:
        copies[name].wait()

    term = jnp.zeros((1, LANES), f32)
    for k in colors:
        arrive(power_sent[k])
        packed = add_slots(power_slots.at[k], src_devices)
        turned = pltpu.roll(packed, HALF, 1)
        coarse = jnp.concatenate(
            [jnp.where(low_half, packed, turned), jnp.where(low_half, turned, packed)], axis=0
        )
        tall = table_thrice(tables["up_rows"][...], coarse)
        thin = []
        for r in range(0, height, CHUNK):
            part = tall[r : r + CHUNK]
            high = part.astype(bf16)
            wide_high = high.astype(f32)
            mixed = jnp.where(low_half, wide_high, part - wide_high).astype(bf16)
            intensity = mm(jnp.concatenate([mixed, high], axis=1), tables["up_cols"][...])
            level = jnp.tanh((0.5 * steepness) * (intensity - threshold))
            shifted = level + jnp.where(labels[r : r + CHUNK, :] == k + 1, -1.0, 1.0)
            slope = (0.25 * loss_weight * steepness) * shifted * (1.0 - level * level)
            thin.append(times_crossed(slope, tables["down_cols"][...]))
        thin = jnp.concatenate(split(jnp.concatenate(thin, axis=0)), axis=1)
        pair = mm(tables["down_rows"][...], thin)
        slope = pair[:N, :LANES] + pair[N:, :LANES] + pair[:N, LANES:]
        slope = slope + pltpu.roll(slope, HALF, 1)
        term = term + jnp.sum(slope * raw[k], axis=0, keepdims=True)
        if k == 1:
            term_slots[my_clip] = jnp.broadcast_to(0.5 * jnp.sum(term, axis=1, keepdims=True), (8, LANES))
            term_sent = exchange("clip", clip_devices, my_clip, term_slots, term_send, term_recv)

        slope = slope * (weight * (2.0 / (channels * src_devices)))
        field_grad = fields[k] * jnp.concatenate([slope] * channels, axis=1)
        back = table_thrice(tables["field_back"][...], field_grad)
        pieces = []
        for c in range(channels):
            block = back[:, c * LANES : (c + 1) * LANES]
            pieces.append(block[:KP] - rotate(block[KP:]))
        product_grad = add_halves(times_crossed(jnp.concatenate(pieces, axis=0), tables["half_back"][...]))
        along = jnp.zeros((KP, LANES), f32)
        across = jnp.zeros((KP, LANES), f32)
        for c in range(channels):
            block = product_grad[c * KP : (c + 1) * KP]
            along = along + pupil_real[c] * block
            across = across + pupil_imag[c] * block
        window_grad = along - rotate(across)
        padded[k, K - KP : K, :] = pltpu.roll(window_grad, second, 1)
        grad_slots[k, me] = padded[k, pl.ds(K - KP - first, K), :]
        grad_sent.append(
            exchange("src", src_devices, me, grad_slots.at[k], grad_send.at[k], grad_recv.at[k])
        )

    leaving = []
    for k in colors:
        if k == 1:
            for sent in spec_sent + power_sent + grad_sent[:1] + [term_sent]:
                for copy in sent:
                    copy.wait_send()
        arrive(grad_sent[k])
        gathered = add_slots(grad_slots.at[k], src_devices)
        high, low = split(jnp.concatenate([gathered, -rotate(gathered)], axis=0))
        folded = mm(jnp.concatenate([high, low, high], axis=1), tables["col_back"][...])
        pair = mm(tables["row_back"][...], jnp.concatenate(split(folded), axis=0))
        plane = masks[k]
        pull = (4.0 * binarize) * (1.0 - plane * plane) * plane
        result[k] = pair[: result.shape[1]] + pair[result.shape[1] :] - pull
        leaving.append(pltpu.make_async_copy(result.at[k], mask_out.at[k], out_sems.at[k]))
        leaving[-1].start()
        if k == 0:
            arrive(term_sent)
            summed = add_slots(term_slots, clip_devices)
            term_result[0] = jnp.sum(jnp.where(lane == 0, summed[:1], 0.0)) * scale
            leaving.append(pltpu.make_async_copy(term_result, term_out, out_sems.at[2]))
            leaving[-1].start()
    for copy in grad_sent[1]:
        copy.wait_send()
    for copy in leaving:
        copy.wait()


def hand_on(mask_in, term_in, mask_out, term_out, held, term_held, sems):
    colors = range(mask_in.shape[0])
    arriving = [pltpu.make_async_copy(mask_in.at[k], held.at[k], sems.at[k]) for k in colors]
    leaving = [pltpu.make_async_copy(held.at[k], mask_out.at[k], sems.at[2 + k]) for k in colors]
    arriving.append(pltpu.make_async_copy(term_in, term_held, sems.at[4]))
    leaving.append(pltpu.make_async_copy(term_held, term_out, sems.at[5]))
    for copy in arriving:
        copy.start()
    for before, after in zip(arriving, leaving):
        before.wait()
        after.start()
    for copy in leaving:
        copy.wait()


def per_device(color_masks, source_weights, pupil_shifts, pupils, target_labels):
    src_devices = lax.axis_size("src")
    clip_devices = lax.axis_size("clip")
    rows, height = color_masks.shape[2], color_masks.shape[3]
    channels = pupils.shape[0]
    tables = make_tables(height, src_devices)
    masks_here = color_masks[0]
    scale = src_devices / (2.0 * clip_devices * height * height)
    operands = [jnp.asarray(tables[name]) for name in ORDER]
    table_scratch = []
    for name in ORDER:
        shape = tables[name].shape[1:] if name in PER_SOURCE else tables[name].shape
        table_scratch.append(pltpu.VMEM(shape, bf16))
    far = pl.BlockSpec(memory_space=pltpu.HBM)
    dma = pltpu.SemaphoreType.DMA
    mask_grad, terms = pl.pallas_call(
        functools.partial(kernel, src_devices, clip_devices, scale),
        out_shape=(
            jax.ShapeDtypeStruct((2, rows, height), f32),
            jax.ShapeDtypeStruct((1,), f32),
        ),
        in_specs=[far] * (5 + len(ORDER)),
        out_specs=(far, far),
        scratch_shapes=table_scratch
        + [
            pltpu.SMEM((1, 2), jnp.int32),
            pltpu.SMEM((1,), f32),
            pltpu.VMEM((2, rows, height), f32),
            pltpu.VMEM(pupils.shape, f32),
            pltpu.VMEM((height, height), jnp.int32),
            pltpu.VMEM((channels, KP, LANES), f32),
            pltpu.VMEM((channels, KP, LANES), f32),
            pltpu.VMEM((2, N, channels * LANES), f32),
            pltpu.VMEM((2, 2 * K - KP, LANES), f32),
            pltpu.VMEM((2, K, LANES), f32),
            pltpu.VMEM((2, src_devices, K, LANES), f32),
            pltpu.VMEM((2, src_devices, N // 2, LANES), f32),
            pltpu.VMEM((2, src_devices, K, LANES), f32),
            pltpu.VMEM((clip_devices, 8, LANES), f32),
            dma((len(ORDER) + 5,)),
        ]
        + [dma((2, src_devices - 1))] * 6
        + [dma((clip_devices - 1,))] * 2
        + [pltpu.VMEM((2, rows, height), f32), pltpu.SMEM((1,), f32), dma((3,))],
        compiler_params=pltpu.CompilerParams(
            collective_id=0, has_side_effects=True, vmem_limit_bytes=60 * 1024 * 1024
        ),
        name="abbe_gradient",
    )(pupil_shifts, source_weights, masks_here, pupils, target_labels[0], *operands)
    mask_grad, terms = pl.pallas_call(
        hand_on,
        out_shape=(
            jax.ShapeDtypeStruct((2, rows, height), f32),
            jax.ShapeDtypeStruct((1,), f32),
        ),
        in_specs=[far, far],
        out_specs=(far, far),
        scratch_shapes=[pltpu.VMEM((2, rows, height), f32), pltpu.SMEM((1,), f32), dma((6,))],
        compiler_params=pltpu.CompilerParams(vmem_limit_bytes=60 * 1024 * 1024),
        name="hand_on",
    )(mask_grad, terms)
    return mask_grad[None], terms


def solution(mesh):
    in_specs = (P("clip", None, "src", None), P("src"), P("src", None), P(), P("clip", None, None))
    out_specs = (P("clip", None, "src", None), P("src"))
    return jax.shard_map(
        per_device, mesh=mesh, in_specs=in_specs, out_specs=out_specs, check_vma=False
    )
```
